256 devices in a mesh: section: 16 (over x, y), dp: 8 (over z), tensor: 2 (over core).
Axes of the slice: x: 4, y: 4, z: 8, core: 2. Of those that a mesh axis runs over, the one named last changes fastest.
Arguments:
- hidden: bfloat16 [8, 128, 3584], P('dp', 'section', 'tensor'), may hold values from -14 to 14
- head_weight: bfloat16 [3584, 81920], P('tensor', ('section', 'dp')), may hold values from -3 to 3
- teacher_logprobs: float32 [8, 128, 81920], P(None, 'tensor', ('section', 'dp')), may hold values from -40 to 4
- lengths: int32 [8, 4], replicated, may hold values from 1 to 32, 80 in all within a row
Outputs:
- hidden_grad: bfloat16 [8, 128, 3584], P('dp', 'section', 'tensor')
- divergence: float32 [8, 128], P('dp', 'tensor')
The draws below stay inside these ranges and needn't reach their ends.
Inputs may be any that keep to these rules, and one draw needn't show every extreme that they name: Each replica's 4 lengths sum to 80.
All inputs are finite; a program needn't handle non-finite values.
Results may differ from the reference program's by a relative error of at most 0.0051.
Values may be sent and summed in bfloat16 or wider, within the bound.
A program may use at most 64 MiB of HBM per device.

```python
import math
import jax
import jax.numpy as jnp
import numpy as np
from jax import lax

D = 3584
TOK_DEV = 128
MB = 4
SEQ_MB = 32
LIVE = 80
VOCAB = 81920
N_DP = 8


def head_column(key, column_id):
    column_key = jax.random.fold_in(jax.random.fold_in(key, 11), column_id)
    return jnp.clip(jax.random.normal(column_key, (D,), jnp.float32), -5.0, 5.0) * (4.0 / math.sqrt(D))


def draw_head_weight(key, part):
    columns = jax.vmap(lambda column_id: head_column(key, column_id))(jnp.arange(VOCAB, dtype=jnp.int32))
    return columns.T.astype(jnp.bfloat16)


def draw_hidden(key, part):
    key = jax.random.fold_in(key, 3)
    noise_key = jax.random.fold_in(key, 0)
    values = jnp.clip(jax.random.normal(noise_key, (N_DP, TOK_DEV, D), jnp.float32), -6.0, 6.0)
    return values.astype(jnp.bfloat16)


def draw_teacher_logprobs(key, part):
    key = jax.random.fold_in(key, 5)
    noise_key, row_key = jax.random.split(key, 2)
    noise_values = jnp.clip(jax.random.normal(noise_key, (N_DP, TOK_DEV, VOCAB), jnp.float32), -4.0, 4.0)
    offsets = jax.random.uniform(row_key, (N_DP, TOK_DEV, 1), jnp.float32, -1.2, 1.2)
    column_share = jnp.arange(VOCAB, dtype=jnp.int32).astype(jnp.float32) / VOCAB
    values = -math.log(VOCAB) - 2.0 + 2.0 * noise_values + offsets + jnp.log(0.5 + column_share)[None, None, :]
    return values.astype(jnp.float32)


def split_up(number_of, total, bound, skew):
    loads = [(1 << 20) // math.isqrt(rank ** skew) + 1 for rank in range(2, number_of + 1)]
    spare, given = total - bound - (number_of - 1), [1] * (number_of - 1)
    while spare > 0:
        candidates = [i for i in range(number_of - 1) if given[i] < bound]
        pool, left = sum([loads[i] for i in candidates]), spare
        for i in candidates:
            addition = min(bound - given[i], max(1, left * loads[i] // pool), spare)
            given[i] = given[i] + addition
            spare = spare - addition
    return np.array([bound] + given)


def uneven_parts(stream_key, count, total, bound, slope):
    if count == 2:
        one = jax.random.randint(stream_key, (), max(1, total - bound), min(bound, total - 1) + 1)
        return jnp.stack([one, total - one])
    tallies = jnp.asarray(split_up(count, total, bound, slope), jnp.int32)
    pairs = (count - 1) // 2
    giver, receiver = tallies[1:1 + 2 * pairs:2], tallies[2:2 + 2 * pairs:2]
    room = jnp.minimum(giver - 1, bound - receiver)
    moved = jax.random.randint(jax.random.fold_in(stream_key, 1), (pairs,), 0, 1 << 20) % (room + 1)
    tallies = tallies.at[1:1 + 2 * pairs:2].set(giver - moved).at[2:2 + 2 * pairs:2].set(receiver + moved)
    return tallies[jax.random.permutation(jax.random.fold_in(stream_key, 2), count)]


def setup_inputs(seed: int = 0) -> dict:
    key_list = jax.random.split(jax.random.key(seed), 5)
    return {
        "hidden": draw_hidden(jax.random.fold_in(key_list[4], 71), 0),
        "head_weight": draw_head_weight(jax.random.fold_in(key_list[4], 71), 0),
        "teacher_logprobs": draw_teacher_logprobs(jax.random.fold_in(key_list[4], 71), 0),
        "lengths": jax.vmap(lambda own: uneven_parts(own, MB, LIVE, SEQ_MB, 1))(jax.random.split(key_list[3], N_DP)).reshape((N_DP, MB)).astype(jnp.int32),
    }


def replica_terms(hidden_rows, teacher_rows, length_row, head_weight):
    logits = jnp.dot(hidden_rows, head_weight, preferred_element_type=jnp.float32)
    positions = jnp.arange(TOK_DEV, dtype=jnp.int32)
    micro_index = positions // SEQ_MB
    micro_pick = (micro_index[:, None] == jnp.arange(MB, dtype=jnp.int32)[None, :]).astype(jnp.int32)
    chosen = jnp.sum(length_row[None, :] * micro_pick, axis=1)
    live_rows = ((positions % SEQ_MB) < chosen).astype(jnp.float32)
    row_weight = live_rows * (SEQ_MB / chosen.astype(jnp.float32))
    row_top = jnp.max(logits, axis=1)
    exp_total = jnp.sum(jnp.exp(logits - row_top[:, None]), axis=1)
    log_norm = row_top + jnp.log(exp_total)
    teacher_prob = jnp.exp(teacher_rows)
    cross_sum = jnp.sum(teacher_prob * (teacher_rows - logits), axis=1)
    prob_mass = jnp.sum(teacher_prob, axis=1)
    divergence = live_rows * (cross_sum + log_norm * prob_mass)
    logit_grad = (row_weight[:, None] * (jnp.exp(logits - log_norm[:, None]) * prob_mass[:, None] - teacher_prob)).astype(jnp.bfloat16)
    hidden_grad = lax.dot_general(logit_grad, head_weight, (((1,), (1,)), ((), ())), preferred_element_type=jnp.float32).astype(jnp.bfloat16)
    return hidden_grad, divergence


def reference(hidden, head_weight, teacher_logprobs, lengths):
    def per_replica(inputs):
        return replica_terms(inputs[0], inputs[1], inputs[2], head_weight)

    hidden_grad, divergence = lax.map(per_replica, (hidden, teacher_logprobs, lengths))
    return hidden_grad, divergence
```

```python
import jax
import jax.numpy as jnp
from jax import lax
from jax.experimental import pallas as pl
from jax.experimental.pallas import tpu as pltpu
from jax.sharding import PartitionSpec as P

SEQ_MB = 32
NX, NY, NZ = 4, 4, 8
F32, BF16 = jnp.float32, jnp.bfloat16


def kernel(
    hid_ref, w_hbm, tl_hbm, len_ref, grad_ref, div_ref,
    w, tl, tp, zb, hb, lsend, lrecv, lown, stats, rz, ry, rx, g,
    s1, f1, own1, r1h, r1f, tt, s2, r2h, r2f, u, s3, r3,
    lsem, ssem, rsem,
):
    width = w.shape[0]
    half = width // 2
    vocab = w.shape[1]
    section, z, t = lax.axis_index("section"), lax.axis_index("dp"), lax.axis_index("tensor")
    x, y = section // NY, section % NY
    other = 1 - t

    def at_x(k):
        return (((x + k) % NX) * NY + y, z, t)

    def at_y(k):
        return (x * NY + (y + k) % NY, z, t)

    def at_z(k):
        return (section, (z + k) % NZ, t)

    partner = (section, z, other)
    count = [0]

    def send(src, dst, device):
        i = count[0]
        count[0] += 1
        copy = pltpu.make_async_remote_copy(
            src_ref=src, dst_ref=dst, send_sem=ssem.at[i], recv_sem=rsem.at[i],
            device_id=device, device_id_type=pl.DeviceIdType.MESH,
        )
        copy.start()
        started.append(copy)
        return copy

    started = []

    loads = [pltpu.make_async_copy(w_hbm, w, lsem.at[0])]
    for k in range(8):
        loads.append(pltpu.make_async_copy(tl_hbm.at[:, pl.ds(8 * k, 8), :], tl.at[k], lsem.at[k + 1]))
    for load in loads:
        load.start()

    barrier = pltpu.get_barrier_semaphore()
    peers = [at_x(k) for k in range(1, NX)] + [at_y(k) for k in range(1, NY)]
    peers += [at_z(k) for k in range(1, NZ)] + [partner]
    for peer in peers:
        pl.semaphore_signal(barrier, inc=1, device_id=peer, device_id_type=pl.DeviceIdType.MESH)
    pl.semaphore_wait(barrier, len(peers))

    cols = (pl.ds(0, half), pl.ds(half, half))
    copies = [send(hid_ref.at[0], zb.at[z], at_z(k)) for k in (4, 3, 5, 2, 6, 1, 7)]
    zb[z] = hid_ref[0]
    for copy in copies:
        copy.wait_recv()
    hb[x, y] = zb[...].astype(F32).reshape(NZ * 8, width).astype(BF16)

    a_right = send(hb.at[x, y, :, cols[0]], hb.at[x, y, :, cols[0]], at_y(1))
    b_right = send(hb.at[x, y, :, cols[1]], hb.at[x, y, :, cols[1]], at_x(1))
    a_left = send(hb.at[x, y, :, cols[0]], hb.at[x, y, :, cols[0]], at_y(3))
    b_left = send(hb.at[x, y, :, cols[1]], hb.at[x, y, :, cols[1]], at_x(3))
    low, high = pl.ds(0, 32), pl.ds(32, 32)
    y1, y3, x1, x3 = (y + 1) % NY, (y + 3) % NY, (x + 1) % NX, (x + 3) % NX
    a_right.wait_recv()
    c0 = send(hb.at[x, y3, low, cols[0]], hb.at[x, y3, low, cols[0]], at_y(1))
    b_right.wait_recv()
    c1 = send(hb.at[x3, y, low, cols[1]], hb.at[x3, y, low, cols[1]], at_x(1))
    a_left.wait_recv()
    c2 = send(hb.at[x, y1, high, cols[0]], hb.at[x, y1, high, cols[0]], at_y(3))
    b_left.wait_recv()
    c3 = send(hb.at[x1, y, high, cols[1]], hb.at[x1, y, high, cols[1]], at_x(3))
    for copy in (c0, c1, c2, c3):
        copy.wait_recv()

    lo2, hi2 = pl.ds(0, 2), pl.ds(2, 2)

    def a_block(i, part):
        return hb.at[i, part, :, cols[0]]

    def b_block(i, part):
        return hb.at[part, i, :, cols[1]]

    ar0 = send(a_block(x, lo2), a_block(x, lo2), at_x(1))
    br0 = send(b_block(y, lo2), b_block(y, lo2), at_y(1))
    al0 = send(a_block(x, hi2), a_block(x, hi2), at_x(3))
    bl0 = send(b_block(y, hi2), b_block(y, hi2), at_y(3))
    ar1 = send(a_block(x, hi2), a_block(x, hi2), at_x(1))
    br1 = send(b_block(y, hi2), b_block(y, hi2), at_y(1))
    al1 = send(a_block(x, lo2), a_block(x, lo2), at_x(3))
    bl1 = send(b_block(y, lo2), b_block(y, lo2), at_y(3))
    ar0.wait_recv()
    ar2 = send(a_block(x3, lo2), a_block(x3, lo2), at_x(1))
    br0.wait_recv()
    br2 = send(b_block(y3, lo2), b_block(y3, lo2), at_y(1))
    al0.wait_recv()
    al2 = send(a_block(x1, hi2), a_block(x1, hi2), at_x(3))
    bl0.wait_recv()
    bl2 = send(b_block(y1, hi2), b_block(y1, hi2), at_y(3))

    for load in loads:
        load.wait()

    def teacher_block(k, carry):
        tp[k] = jnp.exp(tl[k])
        return carry

    lax.fori_loop(0, 8, teacher_block, 0)

    for copy in (ar1, br1, al1, bl1, ar2, br2, al2, bl2):
        copy.wait_recv()

    exchanges = []
    for j in range(2):
        rows = hb[2 * other + j].reshape(256, width)
        lsend[j] = jnp.dot(rows, w[...], preferred_element_type=F32)
        exchanges.append(send(lsend.at[j], lrecv.at[j], partner))
    for j in range(2):
        rows = hb[2 * t + j].reshape(256, width)
        lown[j] = jnp.dot(rows, w[...], preferred_element_type=F32)

    row_i = lax.broadcasted_iota(jnp.int32, (128, 128), 0)
    lane_i = lax.broadcasted_iota(jnp.int32, (128, 128), 1)
    eye = row_i == lane_i

    def to_lanes(col):
        return jnp.sum(jnp.where(eye, col, 0.0), axis=0, keepdims=True)

    def to_rows(lane):
        return jnp.sum(jnp.where(eye, lane, 0.0), axis=1, keepdims=True)

    for k in range(4):
        j, r = k // 2, (k % 2) * 128
        if k % 2 == 0:
            exchanges[j].wait_recv()
        logits = lown[j, r:r + 128, :] + lrecv[j, r:r + 128, :]
        lown[j, r:r + 128, :] = logits
        teacher = tl[2 * k:2 * k + 2].reshape(128, vocab)
        prob = tp[2 * k:2 * k + 2].reshape(128, vocab)
        top = jnp.max(logits, axis=1, keepdims=True)
        total = jnp.sum(jnp.exp(logits - top), axis=1, keepdims=True)
        cross = jnp.sum(prob * (teacher - logits), axis=1, keepdims=True)
        mass = jnp.sum(prob, axis=1, keepdims=True)
        stats[0, k:k + 1, :] = to_lanes(top)
        stats[0, 4 + k:5 + k, :] = to_lanes(total)
        stats[0, 8 + k:9 + k, :] = to_lanes(cross)
        stats[0, 12 + k:13 + k, :] = to_lanes(mass)

    for level, (slots, at, n) in enumerate(((rz, at_z, NZ), (ry, at_y, NY), (rx, at_x, NX))):
        copies = [send(stats.at[level], slots.at[k - 1], at(k)) for k in range(1, n)]
        for copy in copies:
            copy.wait_recv()
        parts = [stats[level]] + [slots[k] for k in range(n - 1)]
        top = parts[0][0:4]
        for part in parts[1:]:
            top = jnp.maximum(top, part[0:4])
        total = sum(part[4:8] * jnp.exp(part[0:4] - top) for part in parts)
        sums = sum(part[8:16] for part in parts)
        stats[level + 1, 0:4, :] = top
        stats[level + 1, 4:8, :] = total
        stats[level + 1, 8:16, :] = sums

    log_norm = stats[3, 0:4, :] + jnp.log(stats[3, 4:8, :])
    cross, mass = stats[3, 8:12, :], stats[3, 12:16, :]
    row_id = lax.broadcasted_iota(jnp.int32, (4, 128), 0) * 128 + lax.broadcasted_iota(jnp.int32, (4, 128), 1)
    local_section, replica, inner = row_id // 64, (row_id // 8) % 8, row_id % 8
    within = (local_section % 4) * 8 + inner
    micro = local_section // 4
    chosen = jnp.ones((4, 128), jnp.int32)
    for r in range(NZ):
        for m in range(2):
            length = jnp.where(t == 0, len_ref[r, m], len_ref[r, m + 2])
            chosen = jnp.where((replica == r) & (micro == m), length, chosen)
    live = (within < chosen).astype(F32)
    weight = live * (SEQ_MB / chosen.astype(F32))
    divergence = live * (cross + log_norm * mass)
    scale = weight * mass

    div_total = jnp.zeros((1, 128), F32)
    for k in range(4):
        j, r = k // 2, (k % 2) * 128
        norm_rows = to_rows(log_norm[k:k + 1])
        scale_rows = to_rows(scale[k:k + 1])
        weight_rows = to_rows(weight[k:k + 1])
        logits = lown[j, r:r + 128, :]
        prob = tp[2 * k:2 * k + 2].reshape(128, vocab)
        grad = jnp.exp(logits - norm_rows) * scale_rows - weight_rows * prob
        for h in range(2):
            g[2 * t + j, (k % 2) * 2 + h] = grad[64 * h:64 * h + 64].astype(BF16)
        div_rows = to_rows(divergence[k:k + 1])
        place = (2 * k + row_i // 64) * 8 + row_i % 8
        pick = (lane_i == place) & ((row_i // 8) % 8 == z)
        div_total = div_total + jnp.sum(jnp.where(pick, div_rows, 0.0), axis=0, keepdims=True)
    div_ref[...] = div_total[:, 0:64]
    swap = send(g.at[pl.ds(2 * t, 2)], g.at[pl.ds(2 * t, 2)], partner)
    swap.wait_recv()

    def product(part, o):
        if part == 0:
            rows = g[(x + o) % NX]
        else:
            rows = g[:, (y + o) % NY]
        return lax.dot_general(
            rows.reshape(256, vocab), w[pl.ds(part * half, half), :], (((1,), (1,)), ((), ())),
            preferred_element_type=F32,
        ).reshape(4, 64, half)

    first = (at_x, at_y)
    second = (at_y, at_x)
    place2 = (y, x)
    hop, direct = [], []
    for part in range(2):
        s1[part, 2] = product(part, 2).astype(BF16)
        hop.append((
            send(s1.at[part, 2, lo2], r1h.at[part, 0], first[part](1)),
            send(s1.at[part, 2, hi2], r1h.at[part, 1], first[part](3)),
        ))
    for part in range(2):
        block = product(part, 1)
        f1[part, 0] = block[0:2]
        s1[part, 1, 2:4] = block[2:4].astype(BF16)
        direct.append(send(s1.at[part, 1, hi2], r1f.at[part, 0, hi2], first[part](1)))
        block = product(part, 3)
        f1[part, 1] = block[2:4]
        s1[part, 3, 0:2] = block[0:2].astype(BF16)
        direct.append(send(s1.at[part, 3, lo2], r1f.at[part, 1, lo2], first[part](3)))
    for part in range(2):
        hop[part][0].wait_recv()
        s1[part, 1, 0:2] = (f1[part, 0] + r1h[part, 0].astype(F32)).astype(BF16)
        direct.append(send(s1.at[part, 1, lo2], r1f.at[part, 0, lo2], first[part](1)))
        hop[part][1].wait_recv()
        s1[part, 3, 2:4] = (f1[part, 1] + r1h[part, 1].astype(F32)).astype(BF16)
        direct.append(send(s1.at[part, 3, hi2], r1f.at[part, 1, hi2], first[part](3)))
    for part in range(2):
        own1[part] = product(part, 0)
    for copy in direct:
        copy.wait_recv()
    hop, direct = [], []
    for part in range(2):
        def chunk(o):
            i = (place2[part] + o) % 4
            return own1[part, i] + r1f[part, 0, i].astype(F32) + r1f[part, 1, i].astype(F32)

        s2[part, 2] = chunk(2).astype(BF16)
        hop.append((
            send(s2.at[part, 2, low], r2h.at[part, 0], second[part](1)),
            send(s2.at[part, 2, high], r2h.at[part, 1], second[part](3)),
        ))
        tt[part, 1] = chunk(1)
        tt[part, 3] = chunk(3)
        tt[part, 0] = chunk(0)
        s2[part, 1, 32:64] = tt[part, 1, 32:64].astype(BF16)
        direct.append(send(s2.at[part, 1, high], r2f.at[part, 0, high], second[part](1)))
        s2[part, 3, 0:32] = tt[part, 3, 0:32].astype(BF16)
        direct.append(send(s2.at[part, 3, low], r2f.at[part, 1, low], second[part](3)))
    for part in range(2):
        hop[part][0].wait_recv()
        s2[part, 1, 0:32] = (tt[part, 1, 0:32] + r2h[part, 0].astype(F32)).astype(BF16)
        direct.append(send(s2.at[part, 1, low], r2f.at[part, 0, low], second[part](1)))
        hop[part][1].wait_recv()
        s2[part, 3, 32:64] = (tt[part, 3, 32:64] + r2h[part, 1].astype(F32)).astype(BF16)
        direct.append(send(s2.at[part, 3, high], r2f.at[part, 1, high], second[part](3)))
    for copy in direct:
        copy.wait_recv()
    for part in range(2):
        block = tt[part, 0] + r2f[part, 0].astype(F32) + r2f[part, 1].astype(F32)
        u[:, :, part * half:(part + 1) * half] = block.reshape(NZ, 8, half)
    s3[...] = u[...].astype(BF16)
    copies = [send(s3.at[(z + k) % NZ], r3.at[k - 1], at_z(k)) for k in (4, 3, 5, 2, 6, 1, 7)]
    for copy in copies:
        copy.wait_recv()
    total = u[z]
    for k in range(NZ - 1):
        total = total + r3[k].astype(F32)
    grad_ref[0] = total.astype(BF16)

    for copy in started:
        copy.wait_send()


N_SEM = 80


def body(hidden, head_weight, teacher_logprobs, lengths):
    width, vocab = head_weight.shape
    half = width // 2
    V = pltpu.VMEM
    scratch = [
        V((width, vocab), BF16),
        V((8, 8, 8, vocab), F32),
        V((8, 8, 8, vocab), F32),
        V((NZ, 8, width), BF16),
        V((NX, NY, 64, width), BF16),
        V((2, 256, vocab), F32),
        V((2, 256, vocab), F32),
        V((2, 256, vocab), F32),
        V((4, 16, 128), F32),
        V((NZ - 1, 16, 128), F32),
        V((NY - 1, 16, 128), F32),
        V((NX - 1, 16, 128), F32),
        V((NX, NY, 64, vocab), BF16),
        V((2, 4, 4, 64, half), BF16),
        V((2, 2, 2, 64, half), F32),
        V((2, 4, 64, half), F32),
        V((2, 2, 2, 64, half), BF16),
        V((2, 2, 4, 64, half), BF16),
        V((2, 4, 64, half), F32),
        V((2, 4, 64, half), BF16),
        V((2, 2, 32, half), BF16),
        V((2, 2, 64, half), BF16),
        V((NZ, 8, width), F32),
        V((NZ, 8, width), BF16),
        V((NZ - 1, 8, width), BF16),
        pltpu.SemaphoreType.DMA((9,)),
        pltpu.SemaphoreType.DMA((N_SEM,)),
        pltpu.SemaphoreType.DMA((N_SEM,)),
    ]
    return pl.pallas_call(
        kernel,
        out_shape=(
            jax.ShapeDtypeStruct((1, 8, width), BF16),
            jax.ShapeDtypeStruct((1, 64), F32),
        ),
        in_specs=[
            pl.BlockSpec(memory_space=V),
            pl.BlockSpec(memory_space=pl.ANY),
            pl.BlockSpec(memory_space=pl.ANY),
            pl.BlockSpec(memory_space=pltpu.SMEM),
        ],
        out_specs=(pl.BlockSpec(memory_space=V), pl.BlockSpec(memory_space=V)),
        scratch_shapes=scratch,
        compiler_params=pltpu.CompilerParams(
            collective_id=0, has_side_effects=True, vmem_limit_bytes=56 * 1024 * 1024
        ),
        name="distill",
    )(hidden, head_weight, teacher_logprobs, lengths)


def solution(mesh):
    placed = (
        P("dp", "section", "tensor"),
        P("tensor", ("section", "dp")),
        P(None, "tensor", ("section", "dp")),
        P(),
    )
    return jax.shard_map(
        body,
        mesh=mesh,
        in_specs=placed,
        out_specs=(P("dp", "section", "tensor"), P("dp", "tensor")),
        check_vma=False,
    )
```

```python
import jax
import jax.numpy as jnp
from jax import lax
from jax.experimental import pallas as pl
from jax.experimental.pallas import tpu as pltpu
from jax.sharding import PartitionSpec as P

SEQ_MB = 32
NX, NY, NZ = 4, 4, 8
NA, NB = 512, 768
F32, BF16 = jnp.float32, jnp.bfloat16


def kernel(
    hid_ref, w_hbm, tl_hbm, len_hbm, grad_ref, div_ref,
    w, tl, tp, lengths, zb, pb, hb, bz, lsend, lrecv, lown, stats, rz, rp, g,
    s1, f1, own1, r1h, r1f, s2, r2, u, s3, r3, prod, sb, rb, s4, r4,
    lsem, ssem, rsem,
):
    wide = NA + NA
    vocab = w.shape[1]
    section, z, t = lax.axis_index("section"), lax.axis_index("dp"), lax.axis_index("tensor")
    x, y = section // NY, section % NY
    other = 1 - t

    def at_x(k):
        return (((x + k) % NX) * NY + y, z, t)

    def at_y(k):
        return (x * NY + (y + k) % NY, z, t)

    def at_z(k):
        return (section, (z + k) % NZ, t)

    def plane(k):
        return ((x + k // NY) % NX) * NY + (y + k % NY) % NY

    def at_p(k):
        return (plane(k), z, t)

    far_z = (4, 3, 5, 2, 6, 1, 7)
    far_p = (10, 6, 14, 9, 11, 2, 8, 5, 7, 13, 15, 1, 3, 4, 12)
    partner = (section, z, other)
    started = []

    def send(src, dst, device):
        i = len(started)
        copy = pltpu.make_async_remote_copy(
            src_ref=src, dst_ref=dst, send_sem=ssem.at[i], recv_sem=rsem.at[i],
            device_id=device, device_id_type=pl.DeviceIdType.MESH,
        )
        copy.start()
        started.append(copy)
        return copy

    barrier = pltpu.get_barrier_semaphore()
    peers = [at_z(k) for k in far_z] + [at_p(k) for k in far_p] + [partner]
    for peer in peers:
        pl.semaphore_signal(barrier, inc=1, device_id=peer, device_id_type=pl.DeviceIdType.MESH)

    loads = [pltpu.make_async_copy(w_hbm, w, lsem.at[0]), pltpu.make_async_copy(len_hbm, lengths, lsem.at[9])]
    for k in range(8):
        loads.append(pltpu.make_async_copy(tl_hbm.at[:, pl.ds(8 * k, 8), :], tl.at[k], lsem.at[k + 1]))
    for load in loads:
        load.start()
    pl.semaphore_wait(barrier, len(peers))

    ca, cc, cac, cb = pl.ds(0, NA), pl.ds(NA, NA), pl.ds(0, wide), pl.ds(wide, NB)
    zs = [send(hid_ref.at[0, :, cac], zb.at[z], at_z(k)) for k in far_z]
    ps = [send(hid_ref.at[0, :, cb], pb.at[section], at_p(k)) for k in far_p]
    zb[z] = hid_ref[0, :, 0:wide]
    pb[section] = hid_ref[0, :, wide:]
    for copy in zs:
        copy.wait_recv()
    hb[x, y] = zb[...].astype(F32).reshape(NZ * 8, wide).astype(BF16)
    ph2 = []
    for k in (2, 1, 3):
        ph2.append(send(hb.at[x, y, :, ca], hb.at[x, y, :, ca], at_y(k)))
        ph2.append(send(hb.at[x, y, :, cc], hb.at[x, y, :, cc], at_x(k)))
    for copy in ps:
        copy.wait_recv()
    bz[z] = pb[...].astype(F32).reshape(128, NB).astype(BF16)

    top_half, low_half = pl.ds(0, 64), pl.ds(64, 64)

    def b_pass(step, right, rows):
        block = bz.at[(z - step) % NZ if right else (z + step) % NZ, rows]
        return send(block, block, at_z(1 if right else NZ - 1))

    ring = [[b_pass(0, True, top_half), b_pass(0, False, low_half), b_pass(0, True, low_half), b_pass(0, False, top_half)]]

    def b_forward(step, which):
        ring[step - 1][which].wait_recv()
        right = which in (0, 2)
        ring[step].append(b_pass(step, right, top_half if which in (0, 3) else low_half))

    ring.append([])
    for which in range(4):
        b_forward(1, which)

    for copy in ph2:
        copy.wait_recv()
    y1, y3, x1, x3 = (y + 1) % NY, (y + 3) % NY, (x + 1) % NX, (x + 3) % NX
    lo2, hi2 = pl.ds(0, 2), pl.ds(2, 2)

    def a_block(i, part):
        return hb.at[i, part, :, ca]

    def c_block(i, part):
        return hb.at[part, i, :, cc]

    ar0 = send(a_block(x, lo2), a_block(x, lo2), at_x(1))
    br0 = send(c_block(y, lo2), c_block(y, lo2), at_y(1))
    al0 = send(a_block(x, hi2), a_block(x, hi2), at_x(3))
    bl0 = send(c_block(y, hi2), c_block(y, hi2), at_y(3))
    ar1 = send(a_block(x, hi2), a_block(x, hi2), at_x(1))
    br1 = send(c_block(y, hi2), c_block(y, hi2), at_y(1))
    al1 = send(a_block(x, lo2), a_block(x, lo2), at_x(3))
    bl1 = send(c_block(y, lo2), c_block(y, lo2), at_y(3))

    for load in loads:
        load.wait()

    def teacher_block(k, carry):
        tp[k] = jnp.exp(tl[k])
        return carry

    lax.fori_loop(0, 8, teacher_block, 0)

    ring.append([])
    for which in range(4):
        b_forward(2, which)
    ar0.wait_recv()
    ar2 = send(a_block(x3, lo2), a_block(x3, lo2), at_x(1))
    br0.wait_recv()
    br2 = send(c_block(y3, lo2), c_block(y3, lo2), at_y(1))
    al0.wait_recv()
    al2 = send(a_block(x1, hi2), a_block(x1, hi2), at_x(3))
    bl0.wait_recv()
    bl2 = send(c_block(y1, hi2), c_block(y1, hi2), at_y(3))
    ring.append([])
    for which in range(2):
        b_forward(3, which)
    for copy in [ar1, br1, al1, bl1] + ring[2][2:4] + [ar2, br2, al2, bl2] + ring[3]:
        copy.wait_recv()

    w_top, w_low = w[0:wide], w[wide:]

    def b_logits(owner, h):
        rows = pl.ds(64 * owner + 32 * h, 32)
        return jnp.dot(bz[:, rows, :].reshape(256, NB), w_low, preferred_element_type=F32).reshape(8, 4, 8, vocab)

    exchanges = []
    for owner, into in ((other, lsend), (t, lown)):
        for h in range(2):
            rows = hb[2 * owner + h].reshape(256, wide)
            block = jnp.dot(rows, w_top, preferred_element_type=F32).reshape(4, 8, 8, vocab)
            extra = b_logits(owner, h)
            for r in range(NZ):
                into[4 * h:4 * h + 4, r] = block[:, r] + extra[r]
            if into is lsend:
                exchanges.append(send(lsend.at[pl.ds(4 * h, 4)], lrecv.at[pl.ds(4 * h, 4)], partner))

    row_i = lax.broadcasted_iota(jnp.int32, (128, 128), 0)
    lane_i = lax.broadcasted_iota(jnp.int32, (128, 128), 1)
    eye = row_i == lane_i

    def to_lanes(col):
        return jnp.sum(jnp.where(eye, col, 0.0), axis=0, keepdims=True)

    def to_rows(lane):
        return jnp.sum(jnp.where(eye, lane, 0.0), axis=1, keepdims=True)

    for k in range(4):
        if k % 2 == 0:
            exchanges[k // 2].wait_recv()
        pair = slice(2 * k, 2 * k + 2)
        both = lown[pair] + lrecv[pair]
        lown[pair] = both
        logits = both.reshape(128, vocab)
        teacher = tl[pair].reshape(128, vocab)
        prob = tp[pair].reshape(128, vocab)
        top = jnp.max(logits, axis=1, keepdims=True)
        total = jnp.sum(jnp.exp(logits - top), axis=1, keepdims=True)
        cross = jnp.sum(prob * (teacher - logits), axis=1, keepdims=True)
        mass = jnp.sum(prob, axis=1, keepdims=True)
        stats[0, k:k + 1, :] = to_lanes(top)
        stats[0, 4 + k:5 + k, :] = to_lanes(total)
        stats[0, 8 + k:9 + k, :] = to_lanes(cross)
        stats[0, 12 + k:13 + k, :] = to_lanes(mass)

    for level, (slots, at, order) in enumerate(((rz, at_z, far_z), (rp, at_p, far_p))):
        copies = [send(stats.at[level], slots.at[k - 1], at(k)) for k in order]
        for copy in copies:
            copy.wait_recv()
        parts = [stats[level]] + [slots[k] for k in range(len(order))]
        top = parts[0][0:4]
        for part in parts[1:]:
            top = jnp.maximum(top, part[0:4])
        total = sum(part[4:8] * jnp.exp(part[0:4] - top) for part in parts)
        sums = sum(part[8:16] for part in parts)
        stats[level + 1, 0:4, :] = top
        stats[level + 1, 4:8, :] = total
        stats[level + 1, 8:16, :] = sums

    log_norm = stats[2, 0:4, :] + jnp.log(stats[2, 4:8, :])
    cross, mass = stats[2, 8:12, :], stats[2, 12:16, :]
    row_id = lax.broadcasted_iota(jnp.int32, (4, 128), 0) * 128 + lax.broadcasted_iota(jnp.int32, (4, 128), 1)
    local_section, replica, inner = row_id // 64, (row_id // 8) % 8, row_id % 8
    within = (local_section % 4) * 8 + inner
    micro = local_section // 4
    chosen = jnp.ones((4, 128), jnp.int32)
    for r in range(NZ):
        for m in range(2):
            length = jnp.where(t == 0, lengths[r, m], lengths[r, m + 2])
            chosen = jnp.where((replica == r) & (micro == m), length, chosen)
    live = (within < chosen).astype(F32)
    weight = live * (SEQ_MB / chosen.astype(F32))
    divergence = live * (cross + log_norm * mass)
    scale = weight * mass

    div_total = jnp.zeros((1, 128), F32)
    swaps = []
    for k in range(4):
        norm_rows = to_rows(log_norm[k:k + 1])
        scale_rows = to_rows(scale[k:k + 1])
        weight_rows = to_rows(weight[k:k + 1])
        pair = slice(2 * k, 2 * k + 2)
        logits = lown[pair].reshape(128, vocab)
        prob = tp[pair].reshape(128, vocab)
        grad = jnp.exp(logits - norm_rows) * scale_rows - weight_rows * prob
        g[2 * t + k // 2, 2 * (k % 2):2 * (k % 2) + 2] = grad.astype(BF16).reshape(2, 64, vocab)
        mine = g.at[2 * t + k // 2, pl.ds(2 * (k % 2), 2)]
        swaps.append(send(mine, mine, partner))
    for k in range(4):
        div_rows = to_rows(divergence[k:k + 1])
        place = (2 * k + row_i // 64) * 8 + row_i % 8
        pick = (lane_i == place) & ((row_i // 8) % 8 == z)
        div_total = div_total + jnp.sum(jnp.where(pick, div_rows, 0.0), axis=0, keepdims=True)
    div_ref[...] = div_total[:, 0:64]
    for copy in swaps:
        copy.wait_recv()

    def times_w(rows, start, size):
        return lax.dot_general(
            rows, w[start:start + size, :], (((1,), (1,)), ((), ())), preferred_element_type=F32
        )

    def product(part, o):
        rows = g[(x + o) % NX] if part == 0 else g[:, (y + o) % NY]
        return times_w(rows.reshape(256, vocab), part * NA, NA).reshape(4, 64, NA)

    first = (at_x, at_y)
    second = (at_y, at_x)
    hop, direct = [], []
    for part in range(2):
        s1[part, 2] = product(part, 2).astype(BF16)
        hop.append((
            send(s1.at[part, 2, lo2], r1h.at[part, 0], first[part](1)),
            send(s1.at[part, 2, hi2], r1h.at[part, 1], first[part](3)),
        ))
    for i in range(NX):
        block = times_w(g[i].reshape(256, vocab), wide, NB).reshape(4, 8, 8, NB)
        for r in range(NZ):
            prod[r, 32 * i:32 * i + 32] = block[:, r].reshape(32, NB)

    halves = (slice(0, 64), slice(64, 128))

    def b_item(side, item, extra=None):
        step = 0 if item == 0 else (item + 1) // 2
        upper = (item % 2 == 0) if side == 0 else (item % 2 == 1)
        owner = (z + 4 - step) % NZ if side == 0 else (z + 4 + step) % NZ
        value = prod[owner, halves[0 if upper else 1]]
        if extra is not None:
            value = value + extra
        sb[side, item] = value.astype(BF16)
        return send(sb.at[side, item], rb.at[side, item], at_z(1 if side == 0 else NZ - 1))

    sides = [[b_item(side, 0)] for side in range(2)]
    for side in range(2):
        sides[side].append(b_item(side, 1))

    def b_next(item):
        source = 0 if item == 2 else item - 2
        for side in range(2):
            sides[side][source].wait_recv()
            sides[side].append(b_item(side, item, rb[side, source].astype(F32)))

    for part in range(2):
        block = product(part, 1)
        f1[part, 0] = block[0:2]
        s1[part, 1, 2:4] = block[2:4].astype(BF16)
        direct.append(send(s1.at[part, 1, hi2], r1f.at[part, 0, hi2], first[part](1)))
        block = product(part, 3)
        f1[part, 1] = block[2:4]
        s1[part, 3, 0:2] = block[0:2].astype(BF16)
        direct.append(send(s1.at[part, 3, lo2], r1f.at[part, 1, lo2], first[part](3)))
    for part in range(2):
        own1[part] = product(part, 0)
    for part in range(2):
        hop[part][0].wait_recv()
        s1[part, 1, 0:2] = (f1[part, 0] + r1h[part, 0].astype(F32)).astype(BF16)
        direct.append(send(s1.at[part, 1, lo2], r1f.at[part, 0, lo2], first[part](1)))
        hop[part][1].wait_recv()
        s1[part, 3, 2:4] = (f1[part, 1] + r1h[part, 1].astype(F32)).astype(BF16)
        direct.append(send(s1.at[part, 3, hi2], r1f.at[part, 1, hi2], first[part](3)))
    b_next(2)
    b_next(3)
    b_next(4)
    for copy in direct:
        copy.wait_recv()
    place2 = (y, x)
    ph2 = []
    for k in (2, 1, 3):
        for part in range(2):
            i = (place2[part] + k) % 4
            value = own1[part, i] + r1f[part, 0, i].astype(F32) + r1f[part, 1, i].astype(F32)
            s2[part, k - 1] = value.astype(BF16)
            ph2.append(send(s2.at[part, k - 1], r2.at[part, k - 1], second[part](k)))
    b_next(5)
    b_next(6)
    for copy in ph2:
        copy.wait_recv()
    for part in range(2):
        i = place2[part]
        value = own1[part, i] + r1f[part, 0, i].astype(F32) + r1f[part, 1, i].astype(F32)
        for k in range(3):
            value = value + r2[part, k].astype(F32)
        u[:, :, part * NA:(part + 1) * NA] = value.reshape(NZ, 8, NA)
    s3[...] = u[...].astype(BF16)
    zs = [send(s3.at[(z + k) % NZ], r3.at[k - 1], at_z(k)) for k in far_z]
    for side in range(2):
        for item in (5, 6):
            sides[side][item].wait_recv()
    prod[z, halves[0]] = prod[z, halves[0]] + rb[0, 6].astype(F32) + rb[1, 5].astype(F32)
    prod[z, halves[1]] = prod[z, halves[1]] + rb[0, 5].astype(F32) + rb[1, 6].astype(F32)
    s4[...] = prod[z].reshape(16, 8, NB).astype(BF16)
    ps = [send(s4.at[plane(k)], r4.at[k - 1], at_p(k)) for k in far_p]
    for copy in zs:
        copy.wait_recv()
    total = u[z]
    for k in range(NZ - 1):
        total = total + r3[k].astype(F32)
    grad_ref[0, :, 0:wide] = total.astype(BF16)
    for copy in ps:
        copy.wait_recv()
    total = prod[z, pl.ds(pl.multiple_of(8 * section, 8), 8)]
    for k in range(15):
        total = total + r4[k].astype(F32)
    grad_ref[0, :, wide:] = total.astype(BF16)

    for copy in started:
        copy.wait_send()


N_SEM = 160


def body(hidden, head_weight, teacher_logprobs, lengths):
    width, vocab = head_weight.shape
    wide = 2 * NA
    V = pltpu.VMEM
    scratch = [
        V((width, vocab), BF16),
        V((8, 8, 8, vocab), F32),
        V((8, 8, 8, vocab), F32),
        pltpu.SMEM((8, 4), jnp.int32),
        V((NZ, 8, wide), BF16),
        V((16, 8, NB), BF16),
        V((NX, NY, 64, wide), BF16),
        V((NZ, 128, NB), BF16),
        V((8, 8, 8, vocab), F32),
        V((8, 8, 8, vocab), F32),
        V((8, 8, 8, vocab), F32),
        V((3, 16, 128), F32),
        V((NZ - 1, 16, 128), F32),
        V((15, 16, 128), F32),
        V((NX, NY, 64, vocab), BF16),
        V((2, 4, 4, 64, NA), BF16),
        V((2, 2, 2, 64, NA), F32),
        V((2, 4, 64, NA), F32),
        V((2, 2, 2, 64, NA), BF16),
        V((2, 2, 4, 64, NA), BF16),
        V((2, 3, 64, NA), BF16),
        V((2, 3, 64, NA), BF16),
        V((NZ, 8, wide), F32),
        V((NZ, 8, wide), BF16),
        V((NZ - 1, 8, wide), BF16),
        V((NZ, 128, NB), F32),
        V((2, 7, 64, NB), BF16),
        V((2, 7, 64, NB), BF16),
        V((16, 8, NB), BF16),
        V((15, 8, NB), BF16),
        pltpu.SemaphoreType.DMA((10,)),
        pltpu.SemaphoreType.DMA((N_SEM,)),
        pltpu.SemaphoreType.DMA((N_SEM,)),
    ]
    return pl.pallas_call(
        kernel,
        out_shape=(
            jax.ShapeDtypeStruct((1, 8, width), BF16),
            jax.ShapeDtypeStruct((1, 64), F32),
        ),
        in_specs=[
            pl.BlockSpec(memory_space=V),
            pl.BlockSpec(memory_space=pl.ANY),
            pl.BlockSpec(memory_space=pl.ANY),
            pl.BlockSpec(memory_space=pl.ANY),
        ],
        out_specs=(pl.BlockSpec(memory_space=V), pl.BlockSpec(memory_space=V)),
        scratch_shapes=scratch,
        compiler_params=pltpu.CompilerParams(
            collective_id=0, has_side_effects=True, vmem_limit_bytes=56 * 1024 * 1024
        ),
        name="distill",
    )(hidden, head_weight, teacher_logprobs, lengths)


def solution(mesh):
    placed = (
        P("dp", "section", "tensor"),
        P("tensor", ("section", "dp")),
        P(None, "tensor", ("section", "dp")),
        P(),
    )
    return jax.shard_map(
        body,
        mesh=mesh,
        in_specs=placed,
        out_specs=(P("dp", "section", "tensor"), P("dp", "tensor")),
        check_vma=False,
    )
```

```python
import jax
import jax.numpy as jnp
from jax import lax
from jax.experimental import pallas as pl
from jax.experimental.pallas import tpu as pltpu
from jax.sharding import PartitionSpec as P

SEQ_MB = 32
NX, NY, NZ = 4, 4, 8
NA, NB = 512, 768
F32, BF16 = jnp.float32, jnp.bfloat16


def kernel(
    hid_hbm, w_hbm, tl_hbm, len_hbm, grad_ref, div_ref,
    w, tl, tp, lengths, zb, pb, hb, bz, acc, lrecv, stats, rz, rp, g,
    s1, f1, own1, r1h, r1f, s2, r2, u, s3, r3, prod, sb, rb, s4, r4,
    lsem, ssem, rsem,
):
    wide = NA + NA
    vocab = w.shape[1]
    section, z, t = lax.axis_index("section"), lax.axis_index("dp"), lax.axis_index("tensor")
    x, y = section // NY, section % NY
    other = 1 - t

    def at_x(k):
        return (((x + k) % NX) * NY + y, z, t)

    def at_y(k):
        return (x * NY + (y + k) % NY, z, t)

    def at_z(k):
        return (section, (z + k) % NZ, t)

    def plane(k):
        return ((x + k // NY) % NX) * NY + (y + k % NY) % NY

    def at_p(k):
        return (plane(k), z, t)

    far_z = (4, 3, 5, 2, 6, 1, 7)
    far_p = (10, 6, 14, 9, 11, 2, 8, 5, 7, 13, 15, 1, 3, 4, 12)
    partner = (section, z, other)
    started = []

    def send(src, dst, device):
        i = len(started)
        copy = pltpu.make_async_remote_copy(
            src_ref=src, dst_ref=dst, send_sem=ssem.at[i], recv_sem=rsem.at[i],
            device_id=device, device_id_type=pl.DeviceIdType.MESH,
        )
        copy.start()
        started.append(copy)
        return copy

    barrier = pltpu.get_barrier_semaphore()
    peers = [at_z(k) for k in far_z] + [at_p(k) for k in far_p] + [partner]
    for peer in peers:
        pl.semaphore_signal(barrier, inc=1, device_id=peer, device_id_type=pl.DeviceIdType.MESH)

    ca, cc, cac, cb = pl.ds(0, NA), pl.ds(NA, NA), pl.ds(0, wide), pl.ds(wide, NB)
    own_rows = (
        pltpu.make_async_copy(hid_hbm.at[0, :, cac], zb.at[z], lsem.at[10]),
        pltpu.make_async_copy(hid_hbm.at[0, :, cb], pb.at[section], lsem.at[11]),
    )
    for load in own_rows:
        load.start()

    loads = [pltpu.make_async_copy(w_hbm, w, lsem.at[0]), pltpu.make_async_copy(len_hbm, lengths, lsem.at[9])]
    for k in range(8):
        loads.append(pltpu.make_async_copy(tl_hbm.at[:, pl.ds(8 * k, 8), :], tl.at[k], lsem.at[k + 1]))
    for load in loads:
        load.start()
    for load in own_rows:
        load.wait()
    pl.semaphore_wait(barrier, len(peers))

    zs = [send(zb.at[z], zb.at[z], at_z(k)) for k in far_z]
    ps = [send(pb.at[section], pb.at[section], at_p(k)) for k in far_p]
    acc[...] = jnp.zeros_like(acc)
    for copy in zs:
        copy.wait_recv()
    hb[x, y] = zb[...].astype(F32).reshape(NZ * 8, wide).astype(BF16)
    ph2 = []
    for k in (2, 1, 3):
        ph2.append(send(hb.at[x, y, :, ca], hb.at[x, y, :, ca], at_y(k)))
        ph2.append(send(hb.at[x, y, :, cc], hb.at[x, y, :, cc], at_x(k)))
    for copy in ps:
        copy.wait_recv()
    bz[z] = pb[...].astype(F32).reshape(128, NB).astype(BF16)

    top_half, low_half = pl.ds(0, 64), pl.ds(64, 64)

    def b_pass(step, right, rows):
        block = bz.at[(z - step) % NZ if right else (z + step) % NZ, rows]
        return send(block, block, at_z(1 if right else NZ - 1))

    ring = [[b_pass(0, True, top_half), b_pass(0, False, low_half), b_pass(0, True, low_half), b_pass(0, False, top_half)]]

    def b_forward(step, which):
        ring[step - 1][which].wait_recv()
        right = which in (0, 2)
        ring[step].append(b_pass(step, right, top_half if which in (0, 3) else low_half))

    ring.append([])
    for which in range(4):
        b_forward(1, which)

    for copy in ph2:
        copy.wait_recv()
    y1, y3, x1, x3 = (y + 1) % NY, (y + 3) % NY, (x + 1) % NX, (x + 3) % NX
    lo2, hi2 = pl.ds(0, 2), pl.ds(2, 2)

    def a_block(i, part):
        return hb.at[i, part, :, ca]

    def c_block(i, part):
        return hb.at[part, i, :, cc]

    ar0 = send(a_block(x, lo2), a_block(x, lo2), at_x(1))
    br0 = send(c_block(y, lo2), c_block(y, lo2), at_y(1))
    al0 = send(a_block(x, hi2), a_block(x, hi2), at_x(3))
    bl0 = send(c_block(y, hi2), c_block(y, hi2), at_y(3))
    ar1 = send(a_block(x, hi2), a_block(x, hi2), at_x(1))
    br1 = send(c_block(y, hi2), c_block(y, hi2), at_y(1))
    al1 = send(a_block(x, lo2), a_block(x, lo2), at_x(3))
    bl1 = send(c_block(y, lo2), c_block(y, lo2), at_y(3))

    def a_logits(i):
        rows = hb[i, :, :, 0:NA].reshape(256, NA)
        block = jnp.dot(rows, w[0:NA], preferred_element_type=F32)
        acc[i] = acc[i] + block.reshape(4, 8, 8, vocab)

    def c_logits(i):
        rows = hb[:, i, :, NA:wide].reshape(256, NA)
        block = jnp.dot(rows, w[NA:wide], preferred_element_type=F32)
        acc[:, i] = acc[:, i] + block.reshape(4, 8, 8, vocab)

    def b_logits(i):
        block = jnp.dot(bz[i], w[wide:], preferred_element_type=F32)
        acc[:, :, i] = acc[:, :, i] + block.reshape(4, 4, 8, vocab)

    for load in loads:
        load.wait()

    def teacher_block(k, carry):
        tp[k] = jnp.exp(tl[k])
        return carry

    lax.fori_loop(0, 8, teacher_block, 0)
    b_logits(z)
    a_logits(x)
    c_logits(y)

    ring.append([])
    for which in range(4):
        b_forward(2, which)
    b_logits((z + 1) % NZ)
    b_logits((z + 7) % NZ)
    ar0.wait_recv()
    ar2 = send(a_block(x3, lo2), a_block(x3, lo2), at_x(1))
    br0.wait_recv()
    br2 = send(c_block(y3, lo2), c_block(y3, lo2), at_y(1))
    al0.wait_recv()
    al2 = send(a_block(x1, hi2), a_block(x1, hi2), at_x(3))
    bl0.wait_recv()
    bl2 = send(c_block(y1, hi2), c_block(y1, hi2), at_y(3))
    ring.append([])
    for which in range(2):
        b_forward(3, which)
    b_logits((z + 2) % NZ)
    b_logits((z + 6) % NZ)
    for copy in [ar1, br1, al1, bl1]:
        copy.wait_recv()
    for k in (1, 3):
        a_logits((x + k) % NX)
        c_logits((y + k) % NY)
    for copy in ring[2][2:4]:
        copy.wait_recv()
    b_logits((z + 3) % NZ)
    b_logits((z + 5) % NZ)
    for copy in (ar2, al2):
        copy.wait_recv()
    a_logits((x + 2) % NX)
    for copy in (br2, bl2):
        copy.wait_recv()
    c_logits((y + 2) % NY)
    for copy in ring[3]:
        copy.wait_recv()
    b_logits((z + 4) % NZ)
    exchanges = []
    for k in range(4):
        block = acc.at[2 * other + k // 2, pl.ds(2 * (k % 2), 2)]
        exchanges.append(send(block, lrecv.at[pl.ds(2 * k, 2)], partner))

    row_i = lax.broadcasted_iota(jnp.int32, (128, 128), 0)
    lane_i = lax.broadcasted_iota(jnp.int32, (128, 128), 1)
    eye = row_i == lane_i

    def to_lanes(col):
        return jnp.sum(jnp.where(eye, col, 0.0), axis=0, keepdims=True)

    def to_rows(lane):
        return jnp.sum(jnp.where(eye, lane, 0.0), axis=1, keepdims=True)

    for k in range(4):
        exchanges[k].wait_recv()
        pair = slice(2 * k, 2 * k + 2)
        both = acc[2 * t + k // 2, 2 * (k % 2):2 * (k % 2) + 2] + lrecv[pair]
        lrecv[pair] = both
        logits = both.reshape(128, vocab)
        teacher = tl[pair].reshape(128, vocab)
        prob = tp[pair].reshape(128, vocab)
        top = jnp.max(logits, axis=1, keepdims=True)
        total = jnp.sum(jnp.exp(logits - top), axis=1, keepdims=True)
        cross = jnp.sum(prob * (teacher - logits), axis=1, keepdims=True)
        mass = jnp.sum(prob, axis=1, keepdims=True)
        stats[0, k:k + 1, :] = to_lanes(top)
        stats[0, 4 + k:5 + k, :] = to_lanes(total)
        stats[0, 8 + k:9 + k, :] = to_lanes(cross)
        stats[0, 12 + k:13 + k, :] = to_lanes(mass)

    for level, (slots, at, order) in enumerate(((rz, at_z, far_z), (rp, at_p, far_p))):
        copies = [send(stats.at[level], slots.at[k - 1], at(k)) for k in order]
        for copy in copies:
            copy.wait_recv()
        parts = [stats[level]] + [slots[k] for k in range(len(order))]
        top = parts[0][0:4]
        for part in parts[1:]:
            top = jnp.maximum(top, part[0:4])
        total = sum(part[4:8] * jnp.exp(part[0:4] - top) for part in parts)
        sums = sum(part[8:16] for part in parts)
        stats[level + 1, 0:4, :] = top
        stats[level + 1, 4:8, :] = total
        stats[level + 1, 8:16, :] = sums

    log_norm = stats[2, 0:4, :] + jnp.log(stats[2, 4:8, :])
    cross, mass = stats[2, 8:12, :], stats[2, 12:16, :]
    row_id = lax.broadcasted_iota(jnp.int32, (4, 128), 0) * 128 + lax.broadcasted_iota(jnp.int32, (4, 128), 1)
    local_section, replica, inner = row_id // 64, (row_id // 8) % 8, row_id % 8
    within = (local_section % 4) * 8 + inner
    micro = local_section // 4
    chosen = jnp.ones((4, 128), jnp.int32)
    for r in range(NZ):
        for m in range(2):
            length = jnp.where(t == 0, lengths[m, r], lengths[m + 2, r])
            chosen = jnp.where((replica == r) & (micro == m), length, chosen)
    live = (within < chosen).astype(F32)
    weight = live * (SEQ_MB / chosen.astype(F32))
    divergence = live * (cross + log_norm * mass)
    scale = weight * mass

    div_total = jnp.zeros((1, 128), F32)
    swaps = []
    for k in range(4):
        norm_rows = to_rows(log_norm[k:k + 1])
        scale_rows = to_rows(scale[k:k + 1])
        weight_rows = to_rows(weight[k:k + 1])
        pair = slice(2 * k, 2 * k + 2)
        logits = lrecv[pair].reshape(128, vocab)
        prob = tp[pair].reshape(128, vocab)
        grad = jnp.exp(logits - norm_rows) * scale_rows - weight_rows * prob
        g[2 * t + k // 2, 2 * (k % 2):2 * (k % 2) + 2] = grad.reshape(2, 8, 8, vocab).astype(BF16)
        mine = g.at[2 * t + k // 2, pl.ds(2 * (k % 2), 2)]
        swaps.append(send(mine, mine, partner))
    for k in range(4):
        div_rows = to_rows(divergence[k:k + 1])
        place = (2 * k + row_i // 64) * 8 + row_i % 8
        pick = (lane_i == place) & ((row_i // 8) % 8 == z)
        div_total = div_total + jnp.sum(jnp.where(pick, div_rows, 0.0), axis=0, keepdims=True)
    div_ref[...] = div_total[:, 0:64]
    for copy in swaps:
        copy.wait_recv()

    def times_w(rows, start, size):
        return lax.dot_general(
            rows, w[start:start + size, :], (((1,), (1,)), ((), ())), preferred_element_type=F32
        )

    def product(part, o):
        rows = g[(x + o) % NX] if part == 0 else g[:, (y + o) % NY]
        rows = rows.astype(F32).reshape(256, vocab).astype(BF16)
        return times_w(rows, part * NA, NA).reshape(4, 64, NA)

    def b_product(o):
        i = (z + o) % NZ
        rows = g[:, :, i].astype(F32).reshape(128, vocab).astype(BF16)
        prod[i] = times_w(rows, wide, NB)

    first = (at_x, at_y)
    second = (at_y, at_x)
    halves = (slice(0, 64), slice(64, 128))

    def b_item(side, item, extra=None):
        step = 0 if item == 0 else (item + 1) // 2
        upper = (item % 2 == 0) if side == 0 else (item % 2 == 1)
        owner = (z + 4 - step) % NZ if side == 0 else (z + 4 + step) % NZ
        value = prod[owner, halves[0 if upper else 1]]
        if extra is not None:
            value = value + extra
        sb[side, item] = value.astype(BF16)
        return send(sb.at[side, item], rb.at[side, item], at_z(1 if side == 0 else NZ - 1))

    hop, direct = [], []
    b_product(4)
    sides = [[b_item(side, 0)] for side in range(2)]
    for part in range(2):
        s1[part, 2] = product(part, 2).astype(BF16)
        hop.append((
            send(s1.at[part, 2, lo2], r1h.at[part, 0], first[part](1)),
            send(s1.at[part, 2, hi2], r1h.at[part, 1], first[part](3)),
        ))
    for side in range(2):
        b_product((3, 5)[side])
        sides[side].append(b_item(side, 1))

    def b_next(item):
        source = 0 if item == 2 else item - 2
        for side in range(2):
            sides[side][source].wait_recv()
            sides[side].append(b_item(side, item, rb[side, source].astype(F32)))

    for part in range(2):
        block = product(part, 1)
        f1[part, 0] = block[0:2]
        s1[part, 1, 2:4] = block[2:4].astype(BF16)
        direct.append(send(s1.at[part, 1, hi2], r1f.at[part, 0, hi2], first[part](1)))
        block = product(part, 3)
        f1[part, 1] = block[2:4]
        s1[part, 3, 0:2] = block[0:2].astype(BF16)
        direct.append(send(s1.at[part, 3, lo2], r1f.at[part, 1, lo2], first[part](3)))
    b_next(2)
    b_product(2)
    b_product(6)
    for part in range(2):
        hop[part][0].wait_recv()
        s1[part, 1, 0:2] = (f1[part, 0] + r1h[part, 0].astype(F32)).astype(BF16)
        direct.append(send(s1.at[part, 1, lo2], r1f.at[part, 0, lo2], first[part](1)))
        hop[part][1].wait_recv()
        s1[part, 3, 2:4] = (f1[part, 1] + r1h[part, 1].astype(F32)).astype(BF16)
        direct.append(send(s1.at[part, 3, hi2], r1f.at[part, 1, hi2], first[part](3)))
    b_next(3)
    b_product(1)
    b_product(7)
    b_product(0)
    for part in range(2):
        own1[part] = product(part, 0)
    b_next(4)
    b_next(5)
    for copy in direct:
        copy.wait_recv()
    place2 = (y, x)
    ph2 = []
    for k in (2, 1, 3):
        for part in range(2):
            i = (place2[part] + k) % 4
            value = own1[part, i] + r1f[part, 0, i].astype(F32) + r1f[part, 1, i].astype(F32)
            s2[part, k - 1] = value.astype(BF16)
            ph2.append(send(s2.at[part, k - 1], r2.at[part, k - 1], second[part](k)))
    b_next(6)
    for copy in ph2:
        copy.wait_recv()
    for part in range(2):
        i = place2[part]
        value = own1[part, i] + r1f[part, 0, i].astype(F32) + r1f[part, 1, i].astype(F32)
        for k in range(3):
            value = value + r2[part, k].astype(F32)
        u[:, :, part * NA:(part + 1) * NA] = value.reshape(NZ, 8, NA)
    s3[...] = u[...].astype(BF16)
    zs = [send(s3.at[(z + k) % NZ], r3.at[k - 1], at_z(k)) for k in far_z]
    for side in range(2):
        for item in (5, 6):
            sides[side][item].wait_recv()
    prod[z, halves[0]] = prod[z, halves[0]] + rb[0, 6].astype(F32) + rb[1, 5].astype(F32)
    prod[z, halves[1]] = prod[z, halves[1]] + rb[0, 5].astype(F32) + rb[1, 6].astype(F32)
    s4[...] = prod[z].reshape(16, 8, NB).astype(BF16)
    ps = [send(s4.at[plane(k)], r4.at[k - 1], at_p(k)) for k in far_p]
    for copy in zs:
        copy.wait_recv()
    total = u[z]
    for k in range(NZ - 1):
        total = total + r3[k].astype(F32)
    grad_ref[0, :, 0:wide] = total.astype(BF16)
    for copy in ps:
        copy.wait_recv()
    total = prod[z, pl.ds(pl.multiple_of(8 * section, 8), 8)]
    for k in range(15):
        total = total + r4[k].astype(F32)
    grad_ref[0, :, wide:] = total.astype(BF16)

    for copy in started:
        copy.wait_send()


def hand_over(grad_ref, div_ref, grad_out, div_out):
    grad_out[...] = grad_ref[...]
    div_out[...] = div_ref[...]


N_SEM = 160


def body(hidden, head_weight, teacher_logprobs, lengths):
    width, vocab = head_weight.shape
    wide = 2 * NA
    V = pltpu.VMEM
    scratch = [
        V((width, vocab), BF16),
        V((8, 8, 8, vocab), F32),
        V((8, 8, 8, vocab), F32),
        pltpu.SMEM((4, 8), jnp.int32),
        V((NZ, 8, wide), BF16),
        V((16, 8, NB), BF16),
        V((NX, NY, 64, wide), BF16),
        V((NZ, 128, NB), BF16),
        V((NX, NY, 8, 8, vocab), F32),
        V((8, 8, 8, vocab), F32),
        V((3, 16, 128), F32),
        V((NZ - 1, 16, 128), F32),
        V((15, 16, 128), F32),
        V((NX, NY, 8, 8, vocab), BF16),
        V((2, 4, 4, 64, NA), BF16),
        V((2, 2, 2, 64, NA), F32),
        V((2, 4, 64, NA), F32),
        V((2, 2, 2, 64, NA), BF16),
        V((2, 2, 4, 64, NA), BF16),
        V((2, 3, 64, NA), BF16),
        V((2, 3, 64, NA), BF16),
        V((NZ, 8, wide), F32),
        V((NZ, 8, wide), BF16),
        V((NZ - 1, 8, wide), BF16),
        V((NZ, 128, NB), F32),
        V((2, 7, 64, NB), BF16),
        V((2, 7, 64, NB), BF16),
        V((16, 8, NB), BF16),
        V((15, 8, NB), BF16),
        pltpu.SemaphoreType.DMA((12,)),
        pltpu.SemaphoreType.DMA((N_SEM,)),
        pltpu.SemaphoreType.DMA((N_SEM,)),
    ]
    grad, divergence = pl.pallas_call(
        kernel,
        out_shape=(
            jax.ShapeDtypeStruct((1, 8, width), BF16),
            jax.ShapeDtypeStruct((1, 64), F32),
        ),
        in_specs=[
            pl.BlockSpec(memory_space=pl.ANY),
            pl.BlockSpec(memory_space=pl.ANY),
            pl.BlockSpec(memory_space=pl.ANY),
            pl.BlockSpec(memory_space=pl.ANY),
        ],
        out_specs=(pl.BlockSpec(memory_space=V), pl.BlockSpec(memory_space=V)),
        scratch_shapes=scratch,
        compiler_params=pltpu.CompilerParams(
            collective_id=0, has_side_effects=True, vmem_limit_bytes=56 * 1024 * 1024
        ),
        name="distill",
    )(hidden, head_weight, teacher_logprobs, lengths.T)
    return pl.pallas_call(
        hand_over,
        out_shape=(
            jax.ShapeDtypeStruct(grad.shape, grad.dtype),
            jax.ShapeDtypeStruct(divergence.shape, divergence.dtype),
        ),
        in_specs=[pl.BlockSpec(memory_space=V)] * 2,
        out_specs=(pl.BlockSpec(memory_space=V), pl.BlockSpec(memory_space=V)),
        name="hand_over",
    )(grad, divergence)


def solution(mesh):
    placed = (
        P("dp", "section", "tensor"),
        P("tensor", ("section", "dp")),
        P(None, "tensor", ("section", "dp")),
        P(),
    )
    return jax.shard_map(
        body,
        mesh=mesh,
        in_specs=placed,
        out_specs=(P("dp", "section", "tensor"), P("dp", "tensor")),
        check_vma=False,
    )
```

```python
import jax
import jax.numpy as jnp
from jax import lax
from jax.experimental import pallas as pl
from jax.experimental.pallas import tpu as pltpu
from jax.sharding import PartitionSpec as P

SEQ_MB = 32
NX, NY, NZ = 4, 4, 8
NA, NC, NB = 640, 512, 640
F32, BF16 = jnp.float32, jnp.bfloat16


def kernel(
    hid_hbm, w_hbm, tl_hbm, len_hbm, grad_ref, div_ref,
    w, tl, tp, lengths, zb, pb, hb, bz, acc, lrecv, stats, rz, rp, g,
    s1, f1, own1, r1h, sd, r1f, s2, r2, u, s3, r3, prod, sb, rb, s4, r4,
    lsem, ssem, rsem,
):
    wide = NA + NC
    vocab = w.shape[1]
    section, z, t = lax.axis_index("section"), lax.axis_index("dp"), lax.axis_index("tensor")
    x, y = section // NY, section % NY
    other = 1 - t

    def at_x(k):
        return (((x + k) % NX) * NY + y, z, t)

    def at_y(k):
        return (x * NY + (y + k) % NY, z, t)

    def at_z(k):
        return (section, (z + k) % NZ, t)

    def plane(k):
        return ((x + k // NY) % NX) * NY + (y + k % NY) % NY

    def at_p(k):
        return (plane(k), z, t)

    far_z = (4, 3, 5, 2, 6, 1, 7)
    far_p = (10, 6, 14, 9, 11, 2, 8, 5, 7, 13, 15, 1, 3, 4, 12)
    partner = (section, z, other)
    started = []

    def send(src, dst, device):
        i = len(started)
        copy = pltpu.make_async_remote_copy(
            src_ref=src, dst_ref=dst, send_sem=ssem.at[i], recv_sem=rsem.at[i],
            device_id=device, device_id_type=pl.DeviceIdType.MESH,
        )
        copy.start()
        started.append(copy)
        return copy

    barrier = pltpu.get_barrier_semaphore()
    peers = [at_z(k) for k in far_z] + [at_p(k) for k in far_p] + [partner]
    for peer in peers:
        pl.semaphore_signal(barrier, inc=1, device_id=peer, device_id_type=pl.DeviceIdType.MESH)

    ca, cc, cac, cb = pl.ds(0, NA), pl.ds(NA, NC), pl.ds(0, wide), pl.ds(wide, NB)
    own_rows = (
        pltpu.make_async_copy(hid_hbm.at[0, :, cac], zb.at[z], lsem.at[10]),
        pltpu.make_async_copy(hid_hbm.at[0, :, cb], pb.at[section], lsem.at[11]),
    )
    for load in own_rows:
        load.start()

    loads = [pltpu.make_async_copy(w_hbm, w, lsem.at[0]), pltpu.make_async_copy(len_hbm, lengths, lsem.at[9])]
    for k in range(8):
        loads.append(pltpu.make_async_copy(tl_hbm.at[:, pl.ds(8 * k, 8), :], tl.at[k], lsem.at[k + 1]))
    for load in loads:
        load.start()
    for load in own_rows:
        load.wait()
    pl.semaphore_wait(barrier, len(peers))

    zs = [send(zb.at[z], zb.at[z], at_z(k)) for k in far_z]
    ps = [send(pb.at[section], pb.at[section], at_p(k)) for k in far_p]
    acc[...] = jnp.zeros_like(acc)
    for copy in zs:
        copy.wait_recv()
    hb[x, y] = zb[...].astype(F32).reshape(NZ * 8, wide).astype(BF16)

    def a_at(xx, k):
        return hb.at[(x + xx) % NX, (y + k) % NY, :, ca]

    def c_at(yy, k):
        return hb.at[(x + k) % NX, (y + yy) % NY, :, cc]

    blocks = (a_at, c_at)
    along = (at_x, at_y)
    across = (at_y, at_x)

    def odd(part, k):
        return ((y, x)[part] + k) % 2

    spread, near, passed = {}, {}, {}

    def send_near(part, k):
        block = blocks[part](0, k)
        near[part, k] = (send(block, block, along[part](1)), send(block, block, along[part](3)))

    def pass_on(part, k):
        for copy in near[part, k]:
            copy.wait_recv()
        back = 2 * odd(part, k)
        block = blocks[part](3 + back, k)
        passed[part, k] = send(block, block, along[part](1 + back))

    for k in (2, 1, 3):
        for part in range(2):
            block = blocks[part](0, 0)
            spread[part, k] = send(block, block, across[part](k))
    for part in range(2):
        send_near(part, 0)
    for copy in ps:
        copy.wait_recv()
    bz[z] = pb[...].astype(F32).reshape(128, NB).astype(BF16)

    top_half, low_half = pl.ds(0, 64), pl.ds(64, 64)

    def b_pass(step, right, rows):
        block = bz.at[(z - step) % NZ if right else (z + step) % NZ, rows]
        return send(block, block, at_z(1 if right else NZ - 1))

    ring = [[b_pass(0, True, top_half), b_pass(0, False, low_half), b_pass(0, True, low_half), b_pass(0, False, top_half)]]

    def b_forward(step, which):
        ring[step - 1][which].wait_recv()
        right = which in (0, 2)
        ring[step].append(b_pass(step, right, top_half if which in (0, 3) else low_half))

    for k in (1, 3):
        for part in range(2):
            spread[part, k].wait_recv()
            send_near(part, 4 - k)
    ring.append([])
    for which in range(4):
        b_forward(1, which)
    for part in range(2):
        spread[part, 2].wait_recv()
        send_near(part, 2)
    for part in range(2):
        pass_on(part, 0)
    def a_logits(i):
        rows = hb[i, :, :, 0:NA].reshape(256, NA)
        block = jnp.dot(rows, w[0:NA], preferred_element_type=F32)
        acc[i] = acc[i] + block.reshape(4, 8, 8, vocab)

    def c_logits(i):
        rows = hb[:, i, :, NA:wide].reshape(256, NC)
        block = jnp.dot(rows, w[NA:wide], preferred_element_type=F32)
        acc[:, i] = acc[:, i] + block.reshape(4, 8, 8, vocab)

    def b_logits(i):
        block = jnp.dot(bz[i], w[wide:], preferred_element_type=F32)
        acc[:, :, i] = acc[:, :, i] + block.reshape(4, 4, 8, vocab)

    def c_far(owner):
        rows = hb[pl.ds(2 * owner, 2), (y + 2) % NY, :, NA:wide].reshape(128, NC)
        block = jnp.dot(rows, w[NA:wide], preferred_element_type=F32)
        into = acc.at[pl.ds(2 * owner, 2), (y + 2) % NY]
        into[...] = into[...] + block.reshape(2, 8, 8, vocab)

    def b_far(owner):
        rows = bz[(z + 4) % NZ, pl.ds(pl.multiple_of(64 * owner, 64), 64), :]
        block = jnp.dot(rows, w[wide:], preferred_element_type=F32)
        into = acc.at[pl.ds(2 * owner, 2), :, (z + 4) % NZ]
        into[...] = into[...] + block.reshape(2, 4, 8, vocab)

    for load in loads:
        load.wait()

    def teacher_block(k, carry):
        tp[k] = jnp.exp(tl[k])
        return carry

    lax.fori_loop(0, 8, teacher_block, 0)
    b_logits(z)
    a_logits(x)
    c_logits(y)
    for k in (1, 3):
        for part in range(2):
            pass_on(part, k)
    ring.append([])
    for which in range(4):
        b_forward(2, which)
    b_logits((z + 1) % NZ)
    b_logits((z + 7) % NZ)
    for part in range(2):
        pass_on(part, 2)
    for k in (1, 3):
        a_logits((x + k) % NX)
        c_logits((y + k) % NY)
    ring.append([])
    for which in range(2):
        b_forward(3, which)
    b_logits((z + 2) % NZ)
    b_logits((z + 6) % NZ)
    for copy in ring[2][2:4]:
        copy.wait_recv()
    b_logits((z + 3) % NZ)
    b_logits((z + 5) % NZ)
    for k in range(4):
        passed[0, k].wait_recv()
    a_logits((x + 2) % NX)
    for k in range(4):
        passed[1, k].wait_recv()
    for copy in ring[3]:
        copy.wait_recv()
    c_far(other)
    b_far(other)
    exchanges = []
    for k in range(4):
        block = acc.at[2 * other + k // 2, pl.ds(2 * (k % 2), 2)]
        exchanges.append(send(block, lrecv.at[pl.ds(2 * k, 2)], partner))
    c_far(t)
    b_far(t)

    row_i = lax.broadcasted_iota(jnp.int32, (128, 128), 0)
    lane_i = lax.broadcasted_iota(jnp.int32, (128, 128), 1)
    eye = row_i == lane_i

    def to_lanes(col):
        return jnp.sum(jnp.where(eye, col, 0.0), axis=0, keepdims=True)

    def to_rows(lane):
        return jnp.sum(jnp.where(eye, lane, 0.0), axis=1, keepdims=True)

    for k in range(4):
        exchanges[k].wait_recv()
        pair = slice(2 * k, 2 * k + 2)
        both = acc[2 * t + k // 2, 2 * (k % 2):2 * (k % 2) + 2] + lrecv[pair]
        lrecv[pair] = both
        logits = both.reshape(128, vocab)
        teacher = tl[pair].reshape(128, vocab)
        prob = tp[pair].reshape(128, vocab)
        top = jnp.max(logits, axis=1, keepdims=True)
        total = jnp.sum(jnp.exp(logits - top), axis=1, keepdims=True)
        cross = jnp.sum(prob * (teacher - logits), axis=1, keepdims=True)
        mass = jnp.sum(prob, axis=1, keepdims=True)
        stats[0, k:k + 1, :] = to_lanes(top)
        stats[0, 4 + k:5 + k, :] = to_lanes(total)
        stats[0, 8 + k:9 + k, :] = to_lanes(cross)
        stats[0, 12 + k:13 + k, :] = to_lanes(mass)

    for level, (slots, at, order) in enumerate(((rz, at_z, far_z), (rp, at_p, far_p))):
        copies = [send(stats.at[level], slots.at[k - 1], at(k)) for k in order]
        for copy in copies:
            copy.wait_recv()
        parts = [stats[level]] + [slots[k] for k in range(len(order))]
        top = parts[0][0:4]
        for part in parts[1:]:
            top = jnp.maximum(top, part[0:4])
        total = sum(part[4:8] * jnp.exp(part[0:4] - top) for part in parts)
        sums = sum(part[8:16] for part in parts)
        stats[level + 1, 0:4, :] = top
        stats[level + 1, 4:8, :] = total
        stats[level + 1, 8:16, :] = sums

    log_norm = stats[2, 0:4, :] + jnp.log(stats[2, 4:8, :])
    cross, mass = stats[2, 8:12, :], stats[2, 12:16, :]
    row_id = lax.broadcasted_iota(jnp.int32, (4, 128), 0) * 128 + lax.broadcasted_iota(jnp.int32, (4, 128), 1)
    local_section, replica, inner = row_id // 64, (row_id // 8) % 8, row_id % 8
    within = (local_section % 4) * 8 + inner
    micro = local_section // 4
    chosen = jnp.ones((4, 128), jnp.int32)
    for r in range(NZ):
        for m in range(2):
            length = jnp.where(t == 0, lengths[m, r], lengths[m + 2, r])
            chosen = jnp.where((replica == r) & (micro == m), length, chosen)
    live = (within < chosen).astype(F32)
    weight = live * (SEQ_MB / chosen.astype(F32))
    divergence = live * (cross + log_norm * mass)
    scale = weight * mass

    div_total = jnp.zeros((1, 128), F32)
    swaps = []
    for k in range(4):
        norm_rows = to_rows(log_norm[k:k + 1])
        scale_rows = to_rows(scale[k:k + 1])
        weight_rows = to_rows(weight[k:k + 1])
        pair = slice(2 * k, 2 * k + 2)
        logits = lrecv[pair].reshape(128, vocab)
        prob = tp[pair].reshape(128, vocab)
        grad = jnp.exp(logits - norm_rows) * scale_rows - weight_rows * prob
        g[2 * t + k // 2, 2 * (k % 2):2 * (k % 2) + 2] = grad.reshape(2, 8, 8, vocab).astype(BF16)
        mine = g.at[2 * t + k // 2, pl.ds(2 * (k % 2), 2)]
        swaps.append(send(mine, mine, partner))
    for k in range(4):
        div_rows = to_rows(divergence[k:k + 1])
        place = (2 * k + row_i // 64) * 8 + row_i % 8
        pick = (lane_i == place) & ((row_i // 8) % 8 == z)
        div_total = div_total + jnp.sum(jnp.where(pick, div_rows, 0.0), axis=0, keepdims=True)
    div_ref[...] = div_total[:, 0:64]
    for copy in swaps:
        copy.wait_recv()

    def times_w(rows, start, size):
        return lax.dot_general(
            rows, w[start:start + size, :], (((1,), (1,)), ((), ())), preferred_element_type=F32
        )

    def product(part, o):
        rows = g[(x + o) % NX] if part == 0 else g[:, (y + o) % NY]
        rows = rows.astype(F32).reshape(256, vocab).astype(BF16)
        return times_w(rows, (0, NA)[part], size[part]).reshape(4, 64, size[part])

    def b_product(o):
        i = (z + o) % NZ
        rows = g[:, :, i].astype(F32).reshape(128, vocab).astype(BF16)
        prod[i] = times_w(rows, wide, NB)

    size = (NA, NC)
    fit = (pl.ds(0, NA), pl.ds(0, NC))
    mine = (y, x)
    order = (2, 1, 3, 0)
    halves = (slice(0, 64), slice(64, 128))

    def b_item(side, item, extra=None):
        step = 0 if item == 0 else (item + 1) // 2
        upper = (item % 2 == 0) if side == 0 else (item % 2 == 1)
        owner = (z + 4 - step) % NZ if side == 0 else (z + 4 + step) % NZ
        value = prod[owner, halves[0 if upper else 1]]
        if extra is not None:
            value = value + extra
        sb[side, item] = value.astype(BF16)
        return send(sb.at[side, item], rb.at[side, item], at_z(1 if side == 0 else NZ - 1))

    hop, direct = {}, {}
    b_product(4)
    sides = [[b_item(side, 0)] for side in range(2)]
    for part in range(2):
        s1[part, :, :, fit[part]] = product(part, 2).astype(BF16)
        for k in order:
            back = 2 * odd(part, k)
            hop[part, k] = send(
                s1.at[part, (mine[part] + k) % 4, :, fit[part]], r1h.at[part, k, :, fit[part]], along[part](1 + back)
            )
    for side in range(2):
        b_product((3, 5)[side])
        sides[side].append(b_item(side, 1))

    def b_next(item):
        source = 0 if item == 2 else item - 2
        for side in range(2):
            sides[side][source].wait_recv()
            sides[side].append(b_item(side, item, rb[side, source].astype(F32)))

    for part in range(2):
        f1[part, 0, :, :, fit[part]] = product(part, 1)
        f1[part, 1, :, :, fit[part]] = product(part, 3)
        for k in order:
            back = odd(part, k)
            sd[part, 0, k, :, fit[part]] = f1[part, 1 - back, (mine[part] + k) % 4, :, fit[part]].astype(BF16)
            direct[part, 0, k] = send(
                sd.at[part, 0, k, :, fit[part]], r1f.at[part, 0, k, :, fit[part]], along[part](3 - 2 * back)
            )
    b_next(2)
    b_product(2)
    b_product(6)
    for k in order:
        for part in range(2):
            hop[part, k].wait_recv()
            back = odd(part, k)
            value = f1[part, back, (mine[part] + k) % 4, :, fit[part]] + r1h[part, k, :, fit[part]].astype(F32)
            sd[part, 1, k, :, fit[part]] = value.astype(BF16)
            direct[part, 1, k] = send(
                sd.at[part, 1, k, :, fit[part]], r1f.at[part, 1, k, :, fit[part]], along[part](1 + 2 * back)
            )
    b_next(3)
    b_product(1)
    b_product(7)
    b_product(0)
    for part in range(2):
        own1[part, :, :, fit[part]] = product(part, 0)
    b_next(4)

    def whole(part, k):
        direct[part, 0, k].wait_recv()
        direct[part, 1, k].wait_recv()
        value = own1[part, (mine[part] + k) % 4, :, fit[part]]
        return value + r1f[part, 0, k, :, fit[part]].astype(F32) + r1f[part, 1, k, :, fit[part]].astype(F32)

    ph2 = []

    def second(k):
        for part in range(2):
            s2[part, k - 1, :, fit[part]] = whole(part, k).astype(BF16)
            ph2.append(send(
                s2.at[part, k - 1, :, fit[part]], r2.at[part, k - 1, :, fit[part]], across[part](k)
            ))

    second(2)
    b_next(5)
    second(1)
    second(3)
    for part in range(2):
        own1[part, mine[part], :, fit[part]] = whole(part, 0)
    b_next(6)
    for copy in ph2:
        copy.wait_recv()
    for part in range(2):
        value = own1[part, mine[part], :, fit[part]]
        for k in range(3):
            value = value + r2[part, k, :, fit[part]].astype(F32)
        start = (0, NA)[part]
        u[:, :, start:start + size[part]] = value.reshape(NZ, 8, size[part])
    s3[...] = u[...].astype(BF16)
    zs = [send(s3.at[(z + k) % NZ], r3.at[k - 1], at_z(k)) for k in far_z]
    for side in range(2):
        for item in (5, 6):
            sides[side][item].wait_recv()
    prod[z, halves[0]] = prod[z, halves[0]] + rb[0, 6].astype(F32) + rb[1, 5].astype(F32)
    prod[z, halves[1]] = prod[z, halves[1]] + rb[0, 5].astype(F32) + rb[1, 6].astype(F32)
    s4[...] = prod[z].reshape(16, 8, NB).astype(BF16)
    ps = [send(s4.at[plane(k)], r4.at[k - 1], at_p(k)) for k in far_p]
    for copy in zs:
        copy.wait_recv()
    total = u[z]
    for k in range(NZ - 1):
        total = total + r3[k].astype(F32)
    grad_ref[0, :, 0:wide] = total.astype(BF16)
    for copy in ps:
        copy.wait_recv()
    total = prod[z, pl.ds(pl.multiple_of(8 * section, 8), 8)]
    for k in range(15):
        total = total + r4[k].astype(F32)
    grad_ref[0, :, wide:] = total.astype(BF16)

    for copy in started:
        copy.wait_send()


def hand_over(grad_ref, div_ref, grad_out, div_out):
    grad_out[...] = grad_ref[...]
    div_out[...] = div_ref[...]


N_SEM = 176


def body(hidden, head_weight, teacher_logprobs, lengths):
    width, vocab = head_weight.shape
    wide = NA + NC
    V = pltpu.VMEM
    scratch = [
        V((width, vocab), BF16),
        V((8, 8, 8, vocab), F32),
        V((8, 8, 8, vocab), F32),
        pltpu.SMEM((4, 8), jnp.int32),
        V((NZ, 8, wide), BF16),
        V((16, 8, NB), BF16),
        V((NX, NY, 64, wide), BF16),
        V((NZ, 128, NB), BF16),
        V((NX, NY, 8, 8, vocab), F32),
        V((8, 8, 8, vocab), F32),
        V((3, 16, 128), F32),
        V((NZ - 1, 16, 128), F32),
        V((15, 16, 128), F32),
        V((NX, NY, 8, 8, vocab), BF16),
        V((2, 4, 64, NA), BF16),
        V((2, 2, 4, 64, NA), F32),
        V((2, 4, 64, NA), F32),
        V((2, 4, 64, NA), BF16),
        V((2, 2, 4, 64, NA), BF16),
        V((2, 2, 4, 64, NA), BF16),
        V((2, 3, 64, NA), BF16),
        V((2, 3, 64, NA), BF16),
        V((NZ, 8, wide), F32),
        V((NZ, 8, wide), BF16),
        V((NZ - 1, 8, wide), BF16),
        V((NZ, 128, NB), F32),
        V((2, 7, 64, NB), BF16),
        V((2, 7, 64, NB), BF16),
        V((16, 8, NB), BF16),
        V((15, 8, NB), BF16),
        pltpu.SemaphoreType.DMA((12,)),
        pltpu.SemaphoreType.DMA((N_SEM,)),
        pltpu.SemaphoreType.DMA((N_SEM,)),
    ]
    grad, divergence = pl.pallas_call(
        kernel,
        out_shape=(
            jax.ShapeDtypeStruct((1, 8, width), BF16),
            jax.ShapeDtypeStruct((1, 64), F32),
        ),
        in_specs=[
            pl.BlockSpec(memory_space=pl.ANY),
            pl.BlockSpec(memory_space=pl.ANY),
            pl.BlockSpec(memory_space=pl.ANY),
            pl.BlockSpec(memory_space=pl.ANY),
        ],
        out_specs=(pl.BlockSpec(memory_space=V), pl.BlockSpec(memory_space=V)),
        scratch_shapes=scratch,
        compiler_params=pltpu.CompilerParams(
            collective_id=0, has_side_effects=True, vmem_limit_bytes=56 * 1024 * 1024
        ),
        name="distill",
    )(hidden, head_weight, teacher_logprobs, lengths.T)
    return pl.pallas_call(
        hand_over,
        out_shape=(
            jax.ShapeDtypeStruct(grad.shape, grad.dtype),
            jax.ShapeDtypeStruct(divergence.shape, divergence.dtype),
        ),
        in_specs=[pl.BlockSpec(memory_space=V)] * 2,
        out_specs=(pl.BlockSpec(memory_space=V), pl.BlockSpec(memory_space=V)),
        name="hand_over",
    )(grad, divergence)


def solution(mesh):
    placed = (
        P("dp", "section", "tensor"),
        P("tensor", ("section", "dp")),
        P(None, "tensor", ("section", "dp")),
        P(),
    )
    return jax.shard_map(
        body,
        mesh=mesh,
        in_specs=placed,
        out_specs=(P("dp", "section", "tensor"), P("dp", "tensor")),
        check_vma=False,
    )
```

```python
import jax
import jax.numpy as jnp
from jax import lax
from jax.experimental import pallas as pl
from jax.experimental.pallas import tpu as pltpu
from jax.sharding import PartitionSpec as P

SEQ_MB, LIVE = 32, 80
NX, NY, NZ = 4, 4, 8
CH, NB = 128, 768
HB = NB // 2
F32, BF16 = jnp.float32, jnp.bfloat16


def kernel(
    hid_hbm, w_hbm, tl_hbm, len_hbm, grad_ref, div_ref,
    w, hid, trow, tlc, tp, lengths, pk, p1, ha, hc, hz, acc, lrecv, stats, rz, rp, dv, g,
    sa, fa, own, rah, sd, raf, s3, r3, prod, sb, rb, pk2, r4, oa, oc,
    lsem, ssem, rsem,
):
    vocab = w.shape[2]
    rows = NZ * LIVE
    section, z, t = lax.axis_index("section"), lax.axis_index("dp"), lax.axis_index("tensor")
    x, y = section // NY, section % NY
    other = 1 - t

    def at_x(k):
        return (((x + k) % NX) * NY + y, z, t)

    def at_y(k):
        return (x * NY + (y + k) % NY, z, t)

    def at_z(k):
        return (section, (z + k) % NZ, t)

    def plane(k):
        return ((x + k // NY) % NX) * NY + (y + k % NY) % NY

    def at_p(k):
        return (plane(k), z, t)

    far_z = (4, 3, 5, 2, 6, 1, 7)
    far_p = (10, 6, 14, 9, 11, 2, 8, 5, 7, 13, 15, 1, 3, 4, 12)
    partner = (section, z, other)
    started = []

    def send(src, dst, device):
        i = len(started)
        copy = pltpu.make_async_remote_copy(
            src_ref=src, dst_ref=dst, send_sem=ssem.at[i], recv_sem=rsem.at[i],
            device_id=device, device_id_type=pl.DeviceIdType.MESH,
        )
        copy.start()
        started.append(copy)
        return copy

    barrier = pltpu.get_barrier_semaphore()
    peers = [at_z(k) for k in far_z] + [at_p(k) for k in far_p] + [partner]
    for peer in peers:
        pl.semaphore_signal(barrier, inc=1, device_id=peer, device_id_type=pl.DeviceIdType.MESH)

    load_hid = pltpu.make_async_copy(hid_hbm.at[0], hid, lsem.at[0])
    load_len = pltpu.make_async_copy(len_hbm, lengths, lsem.at[1])
    load_w = pltpu.make_async_copy(w_hbm, w, lsem.at[2])
    load_tl = pltpu.make_async_copy(tl_hbm.at[pl.ds(4 * t, 4)], trow.at[:, t], lsem.at[3])
    for load in (load_hid, load_len, load_w, load_tl):
        load.start()
    load_hid.wait()
    for p in range(NX * NY):
        a0, c0 = (p // NY) * CH, (NX + p % NY) * CH
        pk[p] = jnp.concatenate([hid[:, a0:a0 + CH], hid[:, c0:c0 + CH], hid[:, 8 * CH:]], axis=1)
    pl.semaphore_wait(barrier, len(peers))

    ps = [send(pk.at[plane(k)], p1.at[section], at_p(k)) for k in far_p]
    teacher_swap = send(tl_hbm.at[pl.ds(4 * other, 4)], trow.at[:, t], partner)
    p1[section] = pk[section]
    acc[...] = jnp.zeros_like(acc)
    load_len.wait()

    def ends(r):
        first = lengths[0, r]
        second = first + lengths[1, r]
        return first, second, second + lengths[2, r]

    def position(r, j):
        e1, e2, e3 = ends(r)
        late = jnp.where(j >= e3, 3 * SEQ_MB - e3, 2 * SEQ_MB - e2)
        early = jnp.where(j >= e1, SEQ_MB - e1, 0)
        return j + jnp.where(j >= e2, late, early)

    row_j = lax.broadcasted_iota(jnp.int32, (LIVE, 128), 0)
    lane_p = lax.broadcasted_iota(jnp.int32, (LIVE, 128), 1)
    eye = row_j == lane_p

    def picker(r):
        return (lane_p == position(r, row_j)).astype(F32).astype(BF16)

    pick_z = picker(z)
    for copy in ps:
        copy.wait_recv()
    block = p1[...].astype(F32).reshape(128, 2 * CH + NB).astype(BF16)
    block = jnp.dot(pick_z, block, preferred_element_type=F32).astype(BF16)
    ha[x, z] = block[:, 0:CH]
    hc[y, z] = block[:, CH:2 * CH]
    hz[z] = block[:, 2 * CH:]

    def b_pass(step, right):
        i = (z - step) % NZ if right else (z + step) % NZ
        part = hz.at[i] if step < 3 else hz.at[i, :, pl.ds(0 if right else HB, HB)]
        return send(part, part, at_z(1 if right else NZ - 1))

    ring = [(b_pass(0, True), b_pass(0, False))]
    zs = []
    for k in far_z:
        zs.append(send(ha.at[x, z], ha.at[x, z], at_z(k)))
        zs.append(send(hc.at[y, z], hc.at[y, z], at_z(k)))

    def b_forward(step):
        ring[step - 1][0].wait_recv()
        right = b_pass(step, True)
        ring[step - 1][1].wait_recv()
        ring.append((right, b_pass(step, False)))

    load_w.wait()

    def b_logits(i):
        low = w[2 * NX:].reshape(NB, vocab)
        acc[i] = acc[i] + jnp.dot(hz[i], low, preferred_element_type=F32)

    def ac_logits(chunks, start, count):
        left = [ha[(x + k) % NX, pl.ds(start, count)].reshape(count * LIVE, CH) for k in chunks]
        left += [hc[(y + k) % NY, pl.ds(start, count)].reshape(count * LIVE, CH) for k in chunks]
        right = [w[(x + k) % NX] for k in chunks] + [w[NX + (y + k) % NY] for k in chunks]
        block = jnp.dot(
            jnp.concatenate(left, axis=1), jnp.concatenate(right, axis=0), preferred_element_type=F32
        )
        into = acc.at[pl.ds(start, count)]
        into[...] = into[...] + block.reshape(count, LIVE, vocab)

    load_tl.wait()
    teacher_swap.wait_recv()
    for r in range(4):
        pick = picker(4 * t + r)
        rest = trow[r].reshape(128, vocab)
        total = None
        for _ in range(3):
            piece = rest.astype(BF16)
            rest = rest - piece.astype(F32)
            part = jnp.dot(pick, piece, preferred_element_type=F32)
            total = part if total is None else total + part
        tlc[r] = total
        tp[r] = jnp.exp(total)

    b_forward(1)
    b_logits(z)
    for copy in zs:
        copy.wait_recv()
    near = (
        send(ha.at[x], ha.at[x], at_x(1)), send(hc.at[y], hc.at[y], at_y(1)),
        send(ha.at[x], ha.at[x], at_x(3)), send(hc.at[y], hc.at[y], at_y(3)),
    )
    b_logits((z + 1) % NZ)
    b_logits((z + 7) % NZ)
    b_forward(2)
    b_logits((z + 2) % NZ)
    b_logits((z + 6) % NZ)
    upper, lower = pl.ds(0, 4), pl.ds(4, 4)
    x1, x3, y1, y3 = (x + 1) % NX, (x + 3) % NX, (y + 1) % NY, (y + 3) % NY
    passed = []
    for copy, buf, i, half, device in (
        (near[0], ha, x3, upper, at_x(1)), (near[1], hc, y3, upper, at_y(1)),
        (near[2], ha, x1, lower, at_x(3)), (near[3], hc, y1, lower, at_y(3)),
    ):
        copy.wait_recv()
        passed.append(send(buf.at[i, half], buf.at[i, half], device))
    b_forward(3)
    ac_logits((0, 1, 3), 0, NZ)
    b_logits((z + 3) % NZ)
    b_logits((z + 5) % NZ)
    for copy in passed:
        copy.wait_recv()
    ac_logits((2,), 4 * other, 4)
    for copy in ring[3]:
        copy.wait_recv()
    b_logits((z + 4) % NZ)
    exchanges = []
    for k in range(4):
        exchanges.append(send(acc.at[4 * other + k], lrecv.at[k], partner))
    ac_logits((2,), 4 * t, 4)

    def to_lanes(col):
        return jnp.sum(jnp.where(eye, col, 0.0), axis=0, keepdims=True)

    def to_rows(lane):
        return jnp.sum(jnp.where(eye, lane, 0.0), axis=1, keepdims=True)

    for k in range(4):
        exchanges[k].wait_recv()
        logits = acc[4 * t + k] + lrecv[k]
        lrecv[k] = logits
        prob = tp[k]
        top = jnp.max(logits, axis=1, keepdims=True)
        total = jnp.sum(jnp.exp(logits - top), axis=1, keepdims=True)
        cross = jnp.sum(prob * (tlc[k] - logits), axis=1, keepdims=True)
        mass = jnp.sum(prob, axis=1, keepdims=True)
        stats[0, k:k + 1, :] = to_lanes(top)
        stats[0, 4 + k:5 + k, :] = to_lanes(total)
        stats[0, 8 + k:9 + k, :] = to_lanes(cross)
        stats[0, 12 + k:13 + k, :] = to_lanes(mass)

    for level, (slots, at, order) in enumerate(((rz, at_z, far_z), (rp, at_p, far_p))):
        copies = [send(stats.at[level], slots.at[k - 1], at(k)) for k in order]
        for copy in copies:
            copy.wait_recv()
        parts = [stats[level]] + [slots[k] for k in range(len(order))]
        top = parts[0][0:4]
        for part in parts[1:]:
            top = jnp.maximum(top, part[0:4])
        total = sum(part[4:8] * jnp.exp(part[0:4] - top) for part in parts)
        sums = sum(part[8:16] for part in parts)
        stats[level + 1, 0:4, :] = top
        stats[level + 1, 4:8, :] = total
        stats[level + 1, 8:16, :] = sums

    row_r = lax.broadcasted_iota(jnp.int32, (4, 128), 0)
    lane_j = lax.broadcasted_iota(jnp.int32, (4, 128), 1)
    log_norm = stats[2, 0:4, :] + jnp.log(jnp.where(lane_j < LIVE, stats[2, 4:8, :], 1.0))
    cross, mass = stats[2, 8:12, :], stats[2, 12:16, :]
    chosen = jnp.ones((4, 128), jnp.int32)
    for r in range(4):
        e1, e2, e3 = ends(4 * t + r)
        late = jnp.where(lane_j >= e3, lengths[3, 4 * t + r], lengths[2, 4 * t + r])
        early = jnp.where(lane_j >= e1, lengths[1, 4 * t + r], lengths[0, 4 * t + r])
        chosen = jnp.where(row_r == r, jnp.where(lane_j >= e2, late, early), chosen)
    weight = SEQ_MB / chosen.astype(F32)
    dv[t] = cross + log_norm * mass
    scale = weight * mass

    swaps = []
    for k in range(4):
        norm_rows = to_rows(log_norm[k:k + 1])
        scale_rows = to_rows(scale[k:k + 1])
        weight_rows = to_rows(weight[k:k + 1])
        grad = jnp.exp(lrecv[k] - norm_rows) * scale_rows - weight_rows * tp[k]
        g[4 * t + k] = grad.astype(BF16)
        swaps.append(send(g.at[4 * t + k], g.at[4 * t + k], partner))
    share = send(dv.at[t], dv.at[t], partner)
    for copy in swaps:
        copy.wait_recv()

    def times_w(left, right):
        return lax.dot_general(left, right, (((1,), (1,)), ((), ())), preferred_element_type=F32)

    def product(part, o):
        chunk = w[(x + o) % NX] if part == 0 else w[NX + (y + o) % NY]
        return times_w(g[...].reshape(rows, vocab), chunk)

    along = (at_x, at_y)
    cut = rows // 2

    def b_item(side, item, extra=None):
        step = 0 if item == 0 else (item + 1) // 2
        first = (item % 2 == 0) if side == 0 else (item % 2 == 1)
        owner = (z + 4 - step) % NZ if side == 0 else (z + 4 + step) % NZ
        value = prod[owner, :, 0:HB] if first else prod[owner, :, HB:NB]
        if extra is not None:
            value = value + extra
        sb[side, item] = value.astype(BF16)
        return send(sb.at[side, item], rb.at[side, item], at_z(1 if side == 0 else NZ - 1))

    def b_next(item):
        source = item - 2
        for side in range(2):
            sides[side][source].wait_recv()
            sides[side].append(b_item(side, item, rb[side, source].astype(F32)))

    low = w[2 * NX:].reshape(NB, vocab)
    prod[(z + 4) % NZ] = times_w(g[(z + 4) % NZ], low)
    sides = [[b_item(side, 0)] for side in range(2)]
    hop, direct = [], []
    for part in range(2):
        sa[part] = product(part, 2).astype(BF16)
        hop.append((
            send(sa.at[part, pl.ds(0, cut)], rah.at[part, 0], along[part](1)),
            send(sa.at[part, pl.ds(cut, cut)], rah.at[part, 1], along[part](3)),
        ))
    prod[...] = times_w(g[...].reshape(rows, vocab), low).reshape(NZ, LIVE, NB)
    for side in range(2):
        sides[side].append(b_item(side, 1))
    for part in range(2):
        for d, o in ((0, 1), (1, 3)):
            block = product(part, o)
            fa[part, d] = block[d * cut:(d + 1) * cut]
            sd[part, d, 1 - d] = block[(1 - d) * cut:(2 - d) * cut].astype(BF16)
            direct.append(send(sd.at[part, d, 1 - d], raf.at[part, d, 1 - d], along[part](o)))
    b_next(2)
    for part in range(2):
        own[part] = product(part, 0)
    for part in range(2):
        for d, o in ((0, 1), (1, 3)):
            hop[part][d].wait_recv()
            sd[part, d, d] = (fa[part, d] + rah[part, d].astype(F32)).astype(BF16)
            direct.append(send(sd.at[part, d, d], raf.at[part, d, d], along[part](o)))
    b_next(3)
    b_next(4)
    for copy in direct:
        copy.wait_recv()
    for part in range(2):
        for h in range(2):
            piece = pl.ds(h * cut, cut)
            value = own[part, piece] + raf[part, 0, h].astype(F32) + raf[part, 1, h].astype(F32)
            own[part, piece] = value
            s3[4 * h:4 * h + 4, :, part * CH:(part + 1) * CH] = value.reshape(4, LIVE, CH).astype(BF16)
    zs = [send(s3.at[(z + k) % NZ], r3.at[k - 1], at_z(k)) for k in far_z]
    b_next(5)
    b_next(6)
    share.wait_recv()
    mine = jnp.sum(jnp.where(row_r == z % 4, dv[z // 4], 0.0), axis=0, keepdims=True)
    placed = lane_p + 64 * t == position(z, row_j)
    div_ref[...] = jnp.sum(jnp.where(placed, to_rows(mine), 0.0), axis=0, keepdims=True)[:, 0:64]
    for side in range(2):
        for item in (5, 6):
            sides[side][item].wait_recv()
    b_first = prod[z, :, 0:HB] + rb[0, 6].astype(F32) + rb[1, 5].astype(F32)
    b_second = prod[z, :, HB:NB] + rb[0, 5].astype(F32) + rb[1, 6].astype(F32)
    for copy in zs:
        copy.wait_recv()
    start = pl.multiple_of(z * LIVE, LIVE)
    ac = jnp.concatenate([own[0, pl.ds(start, LIVE)], own[1, pl.ds(start, LIVE)]], axis=1)
    for k in range(NZ - 1):
        ac = ac + r3[k].astype(F32)
    live = jnp.concatenate([ac.astype(BF16), b_first.astype(BF16), b_second.astype(BF16)], axis=1)
    spread_p = lax.broadcasted_iota(jnp.int32, (128, LIVE), 0)
    spread_j = lax.broadcasted_iota(jnp.int32, (128, LIVE), 1)
    spread = (spread_p == position(z, spread_j)).astype(F32).astype(BF16)
    full = jnp.dot(spread, live, preferred_element_type=F32)
    pk2[...] = full.reshape(NX * NY, 8, 2 * CH + NB).astype(BF16)
    ps = [send(pk2.at[plane(k)], r4.at[k - 1], at_p(k)) for k in far_p]
    for copy in ps:
        copy.wait_recv()
    parts = [pk2[section].astype(F32)] + [r4[k].astype(F32) for k in range(15)]
    for i in range(4):
        oa[(x + NX - i) % NX] = sum(parts[NY * i + j][:, 0:CH] for j in range(4))
        oc[(y + NY - i) % NY] = sum(parts[NY * j + i][:, CH:2 * CH] for j in range(4))
    grad_ref[0, :, 2 * NX * CH:] = sum(part[:, 2 * CH:] for part in parts).astype(BF16)
    for i in range(4):
        grad_ref[0, :, i * CH:(i + 1) * CH] = oa[i].astype(BF16)
        grad_ref[0, :, (NX + i) * CH:(NX + i + 1) * CH] = oc[i].astype(BF16)

    for copy in started:
        copy.wait_send()


def hand_over(grad_ref, div_ref, grad_out, div_out):
    grad_out[...] = grad_ref[...]
    div_out[...] = div_ref[...]


N_SEM = 144


def body(hidden, head_weight, teacher_logprobs, lengths):
    width, vocab = head_weight.shape
    V = pltpu.VMEM
    packed = 2 * CH + NB
    rows = NZ * LIVE
    scratch = [
        V((width // CH, CH, vocab), BF16),
        V((8, width), BF16),
        V((4, 2, 64, vocab), F32),
        V((4, LIVE, vocab), F32),
        V((4, LIVE, vocab), F32),
        pltpu.SMEM((4, 8), jnp.int32),
        V((16, 8, packed), BF16),
        V((16, 8, packed), BF16),
        V((NX, NZ, LIVE, CH), BF16),
        V((NY, NZ, LIVE, CH), BF16),
        V((NZ, LIVE, NB), BF16),
        V((NZ, LIVE, vocab), F32),
        V((4, LIVE, vocab), F32),
        V((3, 16, 128), F32),
        V((NZ - 1, 16, 128), F32),
        V((15, 16, 128), F32),
        V((2, 4, 128), F32),
        V((NZ, LIVE, vocab), BF16),
        V((2, rows, CH), BF16),
        V((2, 2, rows // 2, CH), F32),
        V((2, rows, CH), F32),
        V((2, 2, rows // 2, CH), BF16),
        V((2, 2, 2, rows // 2, CH), BF16),
        V((2, 2, 2, rows // 2, CH), BF16),
        V((NZ, LIVE, 2 * CH), BF16),
        V((NZ - 1, LIVE, 2 * CH), BF16),
        V((NZ, LIVE, NB), F32),
        V((2, 7, LIVE, HB), BF16),
        V((2, 7, LIVE, HB), BF16),
        V((16, 8, packed), BF16),
        V((15, 8, packed), BF16),
        V((NX, 8, CH), F32),
        V((NY, 8, CH), F32),
        pltpu.SemaphoreType.DMA((4,)),
        pltpu.SemaphoreType.DMA((N_SEM,)),
        pltpu.SemaphoreType.DMA((N_SEM,)),
    ]
    grad, divergence = pl.pallas_call(
        kernel,
        out_shape=(
            jax.ShapeDtypeStruct((1, 8, width), BF16),
            jax.ShapeDtypeStruct((1, 64), F32),
        ),
        in_specs=[
            pl.BlockSpec(memory_space=pl.ANY),
            pl.BlockSpec(memory_space=pl.ANY),
            pl.BlockSpec(memory_space=pl.ANY),
            pl.BlockSpec(memory_space=pl.ANY),
        ],
        out_specs=(pl.BlockSpec(memory_space=V), pl.BlockSpec(memory_space=V)),
        scratch_shapes=scratch,
        compiler_params=pltpu.CompilerParams(
            collective_id=0, has_side_effects=True, vmem_limit_bytes=56 * 1024 * 1024
        ),
        name="distill",
    )(hidden, head_weight.reshape(width // CH, CH, vocab), teacher_logprobs, lengths.T)
    return pl.pallas_call(
        hand_over,
        out_shape=(
            jax.ShapeDtypeStruct(grad.shape, grad.dtype),
            jax.ShapeDtypeStruct(divergence.shape, divergence.dtype),
        ),
        in_specs=[pl.BlockSpec(memory_space=V)] * 2,
        out_specs=(pl.BlockSpec(memory_space=V), pl.BlockSpec(memory_space=V)),
        name="hand_over",
    )(grad, divergence)


def solution(mesh):
    placed = (
        P("dp", "section", "tensor"),
        P("tensor", ("section", "dp")),
        P(None, "tensor", ("section", "dp")),
        P(),
    )
    return jax.shard_map(
        body,
        mesh=mesh,
        in_specs=placed,
        out_specs=(P("dp", "section", "tensor"), P("dp", "tensor")),
        check_vma=False,
    )
```

```python
import jax
import jax.numpy as jnp
from jax import lax
from jax.experimental import pallas as pl
from jax.experimental.pallas import tpu as pltpu
from jax.sharding import PartitionSpec as P

SEQ_MB, LIVE = 32, 80
NX, NY, NZ = 4, 4, 8
NA, NB = 512, 768
HB = NB // 2
F32, BF16 = jnp.float32, jnp.bfloat16


def kernel(
    hid_hbm, w_hbm, tl_hbm, len_hbm, grad_ref, div_ref,
    w, tl, tp, lengths, zb, pb, hb, hz, acc, lrecv, stats, rz, rp, g,
    s1, f1, own1, r1h, r1f, s2, r2, u, s3, r3, prod, sb, rb, s4, r4,
    lsem, ssem, rsem,
):
    wide = NA + NA
    vocab = w.shape[1]
    section, z, t = lax.axis_index("section"), lax.axis_index("dp"), lax.axis_index("tensor")
    x, y = section // NY, section % NY
    other = 1 - t

    def at_x(k):
        return (((x + k) % NX) * NY + y, z, t)

    def at_y(k):
        return (x * NY + (y + k) % NY, z, t)

    def at_z(k):
        return (section, (z + k) % NZ, t)

    def plane(k):
        return ((x + k // NY) % NX) * NY + (y + k % NY) % NY

    def at_p(k):
        return (plane(k), z, t)

    far_z = (4, 3, 5, 2, 6, 1, 7)
    far_p = (10, 6, 14, 9, 11, 2, 8, 5, 7, 13, 15, 1, 3, 4, 12)
    partner = (section, z, other)
    started = []

    def send(src, dst, device):
        i = len(started)
        copy = pltpu.make_async_remote_copy(
            src_ref=src, dst_ref=dst, send_sem=ssem.at[i], recv_sem=rsem.at[i],
            device_id=device, device_id_type=pl.DeviceIdType.MESH,
        )
        copy.start()
        started.append(copy)
        return copy

    barrier = pltpu.get_barrier_semaphore()
    peers = [at_z(k) for k in far_z] + [at_p(k) for k in far_p] + [partner]
    for peer in peers:
        pl.semaphore_signal(barrier, inc=1, device_id=peer, device_id_type=pl.DeviceIdType.MESH)

    ca, cc, cac, cb = pl.ds(0, NA), pl.ds(NA, NA), pl.ds(0, wide), pl.ds(wide, NB)
    own_rows = (
        pltpu.make_async_copy(hid_hbm.at[0, :, cac], zb.at[z], lsem.at[10]),
        pltpu.make_async_copy(hid_hbm.at[0, :, cb], pb.at[section], lsem.at[11]),
    )
    for load in own_rows:
        load.start()

    loads = [pltpu.make_async_copy(w_hbm, w, lsem.at[0]), pltpu.make_async_copy(len_hbm, lengths, lsem.at[9])]
    for k in range(8):
        loads.append(pltpu.make_async_copy(tl_hbm.at[:, pl.ds(8 * k, 8), :], tl.at[k], lsem.at[k + 1]))
    for load in loads:
        load.start()
    for load in own_rows:
        load.wait()
    pl.semaphore_wait(barrier, len(peers))

    zs = [send(zb.at[z], zb.at[z], at_z(k)) for k in far_z]
    ps = [send(pb.at[section], pb.at[section], at_p(k)) for k in far_p]
    acc[...] = jnp.zeros_like(acc)
    loads[1].wait()

    def position(r, j):
        e1 = lengths[0, r]
        e2 = e1 + lengths[1, r]
        e3 = e2 + lengths[2, r]
        late = jnp.where(j >= e3, 3 * SEQ_MB - e3, 2 * SEQ_MB - e2)
        early = jnp.where(j >= e1, SEQ_MB - e1, 0)
        return j + jnp.where(j >= e2, late, early)

    def picked(r, rows):
        j = lax.broadcasted_iota(jnp.int32, (LIVE, 128), 0)
        p = lax.broadcasted_iota(jnp.int32, (LIVE, 128), 1)
        pick = (p == position(r, j)).astype(F32).astype(BF16)
        return jnp.dot(pick, rows, preferred_element_type=F32).astype(BF16)

    def put_back(r, rows):
        p = lax.broadcasted_iota(jnp.int32, (128, LIVE), 0)
        j = lax.broadcasted_iota(jnp.int32, (128, LIVE), 1)
        place = (p == position(r, j)).astype(F32).astype(BF16)
        return jnp.dot(place, rows, preferred_element_type=F32)

    for copy in zs:
        copy.wait_recv()
    hb[x, y] = zb[...].astype(F32).reshape(NZ * 8, wide).astype(BF16)
    ph2 = []
    for k in (2, 1, 3):
        ph2.append(send(hb.at[x, y, :, ca], hb.at[x, y, :, ca], at_y(k)))
        ph2.append(send(hb.at[x, y, :, cc], hb.at[x, y, :, cc], at_x(k)))
    for copy in ps:
        copy.wait_recv()
    hz[z] = picked(z, pb[...].astype(F32).reshape(128, NB).astype(BF16))

    def b_pass(step, right):
        i = (z - step) % NZ if right else (z + step) % NZ
        part = hz.at[i] if step < 3 else hz.at[i, :, pl.ds(0 if right else HB, HB)]
        return send(part, part, at_z(1 if right else NZ - 1))

    ring = [(b_pass(0, True), b_pass(0, False))]

    def b_forward(step):
        ring[step - 1][0].wait_recv()
        right = b_pass(step, True)
        ring[step - 1][1].wait_recv()
        ring.append((right, b_pass(step, False)))

    b_forward(1)

    for copy in ph2:
        copy.wait_recv()
    y1, y3, x1, x3 = (y + 1) % NY, (y + 3) % NY, (x + 1) % NX, (x + 3) % NX
    lo2, hi2 = pl.ds(0, 2), pl.ds(2, 2)

    def a_block(i, part):
        return hb.at[i, part, :, ca]

    def c_block(i, part):
        return hb.at[part, i, :, cc]

    ar0 = send(a_block(x, lo2), a_block(x, lo2), at_x(1))
    br0 = send(c_block(y, lo2), c_block(y, lo2), at_y(1))
    al0 = send(a_block(x, hi2), a_block(x, hi2), at_x(3))
    bl0 = send(c_block(y, hi2), c_block(y, hi2), at_y(3))
    ar1 = send(a_block(x, hi2), a_block(x, hi2), at_x(1))
    br1 = send(c_block(y, hi2), c_block(y, hi2), at_y(1))
    al1 = send(a_block(x, lo2), a_block(x, lo2), at_x(3))
    bl1 = send(c_block(y, lo2), c_block(y, lo2), at_y(3))

    def a_logits(i):
        rows = hb[i, :, :, 0:NA].reshape(256, NA)
        block = jnp.dot(rows, w[0:NA], preferred_element_type=F32)
        acc[i] = acc[i] + block.reshape(4, 8, 8, vocab)

    def c_logits(i):
        rows = hb[:, i, :, NA:wide].reshape(256, NA)
        block = jnp.dot(rows, w[NA:wide], preferred_element_type=F32)
        acc[:, i] = acc[:, i] + block.reshape(4, 8, 8, vocab)

    def b_logits(i):
        rows = put_back(i, hz[i]).astype(BF16)
        block = jnp.dot(rows, w[wide:], preferred_element_type=F32)
        acc[:, :, i] = acc[:, :, i] + block.reshape(4, 4, 8, vocab)

    for load in [loads[0]] + loads[2:]:
        load.wait()

    def teacher_block(k, carry):
        tp[k] = jnp.exp(tl[k])
        return carry

    lax.fori_loop(0, 8, teacher_block, 0)
    b_logits(z)
    a_logits(x)
    c_logits(y)

    b_forward(2)
    b_logits((z + 1) % NZ)
    b_logits((z + 7) % NZ)
    ar0.wait_recv()
    ar2 = send(a_block(x3, lo2), a_block(x3, lo2), at_x(1))
    br0.wait_recv()
    br2 = send(c_block(y3, lo2), c_block(y3, lo2), at_y(1))
    al0.wait_recv()
    al2 = send(a_block(x1, hi2), a_block(x1, hi2), at_x(3))
    bl0.wait_recv()
    bl2 = send(c_block(y1, hi2), c_block(y1, hi2), at_y(3))
    b_forward(3)
    b_logits((z + 2) % NZ)
    b_logits((z + 6) % NZ)
    for copy in [ar1, br1, al1, bl1]:
        copy.wait_recv()
    for k in (1, 3):
        a_logits((x + k) % NX)
        c_logits((y + k) % NY)
    b_logits((z + 3) % NZ)
    b_logits((z + 5) % NZ)
    for copy in (ar2, al2):
        copy.wait_recv()
    a_logits((x + 2) % NX)
    for copy in (br2, bl2):
        copy.wait_recv()
    c_logits((y + 2) % NY)
    for copy in ring[3]:
        copy.wait_recv()
    b_logits((z + 4) % NZ)
    exchanges = []
    for k in range(4):
        block = acc.at[2 * other + k // 2, pl.ds(2 * (k % 2), 2)]
        exchanges.append(send(block, lrecv.at[pl.ds(2 * k, 2)], partner))

    row_i = lax.broadcasted_iota(jnp.int32, (128, 128), 0)
    lane_i = lax.broadcasted_iota(jnp.int32, (128, 128), 1)
    eye = row_i == lane_i

    def to_lanes(col):
        return jnp.sum(jnp.where(eye, col, 0.0), axis=0, keepdims=True)

    def to_rows(lane):
        return jnp.sum(jnp.where(eye, lane, 0.0), axis=1, keepdims=True)

    for k in range(4):
        exchanges[k].wait_recv()
        pair = slice(2 * k, 2 * k + 2)
        both = acc[2 * t + k // 2, 2 * (k % 2):2 * (k % 2) + 2] + lrecv[pair]
        lrecv[pair] = both
        logits = both.reshape(128, vocab)
        teacher = tl[pair].reshape(128, vocab)
        prob = tp[pair].reshape(128, vocab)
        top = jnp.max(logits, axis=1, keepdims=True)
        total = jnp.sum(jnp.exp(logits - top), axis=1, keepdims=True)
        cross = jnp.sum(prob * (teacher - logits), axis=1, keepdims=True)
        mass = jnp.sum(prob, axis=1, keepdims=True)
        stats[0, k:k + 1, :] = to_lanes(top)
        stats[0, 4 + k:5 + k, :] = to_lanes(total)
        stats[0, 8 + k:9 + k, :] = to_lanes(cross)
        stats[0, 12 + k:13 + k, :] = to_lanes(mass)

    for level, (slots, at, order) in enumerate(((rz, at_z, far_z), (rp, at_p, far_p))):
        copies = [send(stats.at[level], slots.at[k - 1], at(k)) for k in order]
        for copy in copies:
            copy.wait_recv()
        parts = [stats[level]] + [slots[k] for k in range(len(order))]
        top = parts[0][0:4]
        for part in parts[1:]:
            top = jnp.maximum(top, part[0:4])
        total = sum(part[4:8] * jnp.exp(part[0:4] - top) for part in parts)
        sums = sum(part[8:16] for part in parts)
        stats[level + 1, 0:4, :] = top
        stats[level + 1, 4:8, :] = total
        stats[level + 1, 8:16, :] = sums

    log_norm = stats[2, 0:4, :] + jnp.log(stats[2, 4:8, :])
    cross, mass = stats[2, 8:12, :], stats[2, 12:16, :]
    row_id = lax.broadcasted_iota(jnp.int32, (4, 128), 0) * 128 + lax.broadcasted_iota(jnp.int32, (4, 128), 1)
    local_section, replica, inner = row_id // 64, (row_id // 8) % 8, row_id % 8
    within = (local_section % 4) * 8 + inner
    micro = local_section // 4
    chosen = jnp.ones((4, 128), jnp.int32)
    for r in range(NZ):
        for m in range(2):
            length = jnp.where(t == 0, lengths[m, r], lengths[m + 2, r])
            chosen = jnp.where((replica == r) & (micro == m), length, chosen)
    live = (within < chosen).astype(F32)
    weight = live * (SEQ_MB / chosen.astype(F32))
    divergence = live * (cross + log_norm * mass)
    scale = weight * mass

    div_total = jnp.zeros((1, 128), F32)
    swaps = []
    for k in range(4):
        norm_rows = to_rows(log_norm[k:k + 1])
        scale_rows = to_rows(scale[k:k + 1])
        weight_rows = to_rows(weight[k:k + 1])
        pair = slice(2 * k, 2 * k + 2)
        logits = lrecv[pair].reshape(128, vocab)
        prob = tp[pair].reshape(128, vocab)
        grad = jnp.exp(logits - norm_rows) * scale_rows - weight_rows * prob
        g[2 * t + k // 2, 2 * (k % 2):2 * (k % 2) + 2] = grad.reshape(2, 8, 8, vocab).astype(BF16)
        mine = g.at[2 * t + k // 2, pl.ds(2 * (k % 2), 2)]
        swaps.append(send(mine, mine, partner))
    for k in range(4):
        div_rows = to_rows(divergence[k:k + 1])
        place = (2 * k + row_i // 64) * 8 + row_i % 8
        pick = (lane_i == place) & ((row_i // 8) % 8 == z)
        div_total = div_total + jnp.sum(jnp.where(pick, div_rows, 0.0), axis=0, keepdims=True)
    div_ref[...] = div_total[:, 0:64]
    for copy in swaps:
        copy.wait_recv()

    def times_w(rows, start, size):
        return lax.dot_general(
            rows, w[start:start + size, :], (((1,), (1,)), ((), ())), preferred_element_type=F32
        )

    def product(part, o):
        rows = g[(x + o) % NX] if part == 0 else g[:, (y + o) % NY]
        rows = rows.astype(F32).reshape(256, vocab).astype(BF16)
        return times_w(rows, part * NA, NA).reshape(4, 64, NA)

    def b_product(o):
        i = (z + o) % NZ
        rows = g[:, :, i].astype(F32).reshape(128, vocab).astype(BF16)
        prod[i] = times_w(picked(i, rows), wide, NB)

    first = (at_x, at_y)
    second = (at_y, at_x)
    halves = (slice(0, HB), slice(HB, NB))

    def b_item(side, item, extra=None):
        step = 0 if item == 0 else (item + 1) // 2
        upper = (item % 2 == 0) if side == 0 else (item % 2 == 1)
        owner = (z + 4 - step) % NZ if side == 0 else (z + 4 + step) % NZ
        value = prod[owner, :, halves[0 if upper else 1]]
        if extra is not None:
            value = value + extra
        sb[side, item] = value.astype(BF16)
        return send(sb.at[side, item], rb.at[side, item], at_z(1 if side == 0 else NZ - 1))

    hop, direct = [], []
    b_product(4)
    sides = [[b_item(side, 0)] for side in range(2)]
    for part in range(2):
        s1[part, 2] = product(part, 2).astype(BF16)
        hop.append((
            send(s1.at[part, 2, lo2], r1h.at[part, 0], first[part](1)),
            send(s1.at[part, 2, hi2], r1h.at[part, 1], first[part](3)),
        ))
    for side in range(2):
        b_product((3, 5)[side])
        sides[side].append(b_item(side, 1))

    def b_next(item):
        source = 0 if item == 2 else item - 2
        for side in range(2):
            sides[side][source].wait_recv()
            sides[side].append(b_item(side, item, rb[side, source].astype(F32)))

    for part in range(2):
        block = product(part, 1)
        f1[part, 0] = block[0:2]
        s1[part, 1, 2:4] = block[2:4].astype(BF16)
        direct.append(send(s1.at[part, 1, hi2], r1f.at[part, 0, hi2], first[part](1)))
        block = product(part, 3)
        f1[part, 1] = block[2:4]
        s1[part, 3, 0:2] = block[0:2].astype(BF16)
        direct.append(send(s1.at[part, 3, lo2], r1f.at[part, 1, lo2], first[part](3)))
    b_next(2)
    b_product(2)
    b_product(6)
    for part in range(2):
        hop[part][0].wait_recv()
        s1[part, 1, 0:2] = (f1[part, 0] + r1h[part, 0].astype(F32)).astype(BF16)
        direct.append(send(s1.at[part, 1, lo2], r1f.at[part, 0, lo2], first[part](1)))
        hop[part][1].wait_recv()
        s1[part, 3, 2:4] = (f1[part, 1] + r1h[part, 1].astype(F32)).astype(BF16)
        direct.append(send(s1.at[part, 3, hi2], r1f.at[part, 1, hi2], first[part](3)))
    b_next(3)
    b_product(1)
    b_product(7)
    b_product(0)
    for part in range(2):
        own1[part] = product(part, 0)
    b_next(4)
    b_next(5)
    for copy in direct:
        copy.wait_recv()
    place2 = (y, x)
    ph2 = []
    for k in (2, 1, 3):
        for part in range(2):
            i = (place2[part] + k) % 4
            value = own1[part, i] + r1f[part, 0, i].astype(F32) + r1f[part, 1, i].astype(F32)
            s2[part, k - 1] = value.astype(BF16)
            ph2.append(send(s2.at[part, k - 1], r2.at[part, k - 1], second[part](k)))
    b_next(6)
    for copy in ph2:
        copy.wait_recv()
    for part in range(2):
        i = place2[part]
        value = own1[part, i] + r1f[part, 0, i].astype(F32) + r1f[part, 1, i].astype(F32)
        for k in range(3):
            value = value + r2[part, k].astype(F32)
        u[:, :, part * NA:(part + 1) * NA] = value.reshape(NZ, 8, NA)
    s3[...] = u[...].astype(BF16)
    zs = [send(s3.at[(z + k) % NZ], r3.at[k - 1], at_z(k)) for k in far_z]
    for side in range(2):
        for item in (5, 6):
            sides[side][item].wait_recv()
    b_first = prod[z, :, halves[0]] + rb[0, 6].astype(F32) + rb[1, 5].astype(F32)
    b_second = prod[z, :, halves[1]] + rb[0, 5].astype(F32) + rb[1, 6].astype(F32)
    live_rows = jnp.concatenate([b_first.astype(BF16), b_second.astype(BF16)], axis=1)
    s4[...] = put_back(z, live_rows).reshape(16, 8, NB).astype(BF16)
    ps = [send(s4.at[plane(k)], r4.at[k - 1], at_p(k)) for k in far_p]
    for copy in zs:
        copy.wait_recv()
    total = u[z]
    for k in range(NZ - 1):
        total = total + r3[k].astype(F32)
    grad_ref[0, :, 0:wide] = total.astype(BF16)
    for copy in ps:
        copy.wait_recv()
    total = s4[section].astype(F32)
    for k in range(15):
        total = total + r4[k].astype(F32)
    grad_ref[0, :, wide:] = total.astype(BF16)

    for copy in started:
        copy.wait_send()


def hand_over(grad_ref, div_ref, grad_out, div_out):
    grad_out[...] = grad_ref[...]
    div_out[...] = div_ref[...]


N_SEM = 160


def body(hidden, head_weight, teacher_logprobs, lengths):
    width, vocab = head_weight.shape
    wide = 2 * NA
    V = pltpu.VMEM
    scratch = [
        V((width, vocab), BF16),
        V((8, 8, 8, vocab), F32),
        V((8, 8, 8, vocab), F32),
        pltpu.SMEM((4, 8), jnp.int32),
        V((NZ, 8, wide), BF16),
        V((16, 8, NB), BF16),
        V((NX, NY, 64, wide), BF16),
        V((NZ, LIVE, NB), BF16),
        V((NX, NY, 8, 8, vocab), F32),
        V((8, 8, 8, vocab), F32),
        V((3, 16, 128), F32),
        V((NZ - 1, 16, 128), F32),
        V((15, 16, 128), F32),
        V((NX, NY, 8, 8, vocab), BF16),
        V((2, 4, 4, 64, NA), BF16),
        V((2, 2, 2, 64, NA), F32),
        V((2, 4, 64, NA), F32),
        V((2, 2, 2, 64, NA), BF16),
        V((2, 2, 4, 64, NA), BF16),
        V((2, 3, 64, NA), BF16),
        V((2, 3, 64, NA), BF16),
        V((NZ, 8, wide), F32),
        V((NZ, 8, wide), BF16),
        V((NZ - 1, 8, wide), BF16),
        V((NZ, LIVE, NB), F32),
        V((2, 7, LIVE, HB), BF16),
        V((2, 7, LIVE, HB), BF16),
        V((16, 8, NB), BF16),
        V((15, 8, NB), BF16),
        pltpu.SemaphoreType.DMA((12,)),
        pltpu.SemaphoreType.DMA((N_SEM,)),
        pltpu.SemaphoreType.DMA((N_SEM,)),
    ]
    grad, divergence = pl.pallas_call(
        kernel,
        out_shape=(
            jax.ShapeDtypeStruct((1, 8, width), BF16),
            jax.ShapeDtypeStruct((1, 64), F32),
        ),
        in_specs=[
            pl.BlockSpec(memory_space=pl.ANY),
            pl.BlockSpec(memory_space=pl.ANY),
            pl.BlockSpec(memory_space=pl.ANY),
            pl.BlockSpec(memory_space=pl.ANY),
        ],
        out_specs=(pl.BlockSpec(memory_space=V), pl.BlockSpec(memory_space=V)),
        scratch_shapes=scratch,
        compiler_params=pltpu.CompilerParams(
            collective_id=0, has_side_effects=True, vmem_limit_bytes=56 * 1024 * 1024
        ),
        name="distill",
    )(hidden, head_weight, teacher_logprobs, lengths.T)
    return pl.pallas_call(
        hand_over,
        out_shape=(
            jax.ShapeDtypeStruct(grad.shape, grad.dtype),
            jax.ShapeDtypeStruct(divergence.shape, divergence.dtype),
        ),
        in_specs=[pl.BlockSpec(memory_space=V)] * 2,
        out_specs=(pl.BlockSpec(memory_space=V), pl.BlockSpec(memory_space=V)),
        name="hand_over",
    )(grad, divergence)


def solution(mesh):
    placed = (
        P("dp", "section", "tensor"),
        P("tensor", ("section", "dp")),
        P(None, "tensor", ("section", "dp")),
        P(),
    )
    return jax.shard_map(
        body,
        mesh=mesh,
        in_specs=placed,
        out_specs=(P("dp", "section", "tensor"), P("dp", "tensor")),
        check_vma=False,
    )
```

```python
import jax
import jax.numpy as jnp
from jax import lax
from jax.experimental import pallas as pl
from jax.experimental.pallas import tpu as pltpu
from jax.sharding import PartitionSpec as P

SEQ_MB, LIVE = 32, 80
NX, NY, NZ = 4, 4, 8
NA, NC, NB = 512, 512, 768
HB = NB // 2
F32, BF16 = jnp.float32, jnp.bfloat16


def kernel(
    hid_hbm, w_hbm, tl_hbm, len_hbm, grad_ref, div_ref,
    w, tl, tp, lengths, zb, pb, hb, hz, acc, lrecv, stats, rz, rp, g,
    s1, f1, own1, r1h, sd, r1f, s2, r2, u, s3, r3, prod, sb, rb, s4, r4,
    lsem, ssem, rsem,
):
    wide = NA + NC
    vocab = w.shape[1]
    section, z, t = lax.axis_index("section"), lax.axis_index("dp"), lax.axis_index("tensor")
    x, y = section // NY, section % NY
    other = 1 - t

    def at_x(k):
        return (((x + k) % NX) * NY + y, z, t)

    def at_y(k):
        return (x * NY + (y + k) % NY, z, t)

    def at_z(k):
        return (section, (z + k) % NZ, t)

    def plane(k):
        return ((x + k // NY) % NX) * NY + (y + k % NY) % NY

    def at_p(k):
        return (plane(k), z, t)

    far_z = (4, 3, 5, 2, 6, 1, 7)
    far_p = (10, 6, 14, 9, 11, 2, 8, 5, 7, 13, 15, 1, 3, 4, 12)
    partner = (section, z, other)
    started = []

    def send(src, dst, device):
        i = len(started)
        copy = pltpu.make_async_remote_copy(
            src_ref=src, dst_ref=dst, send_sem=ssem.at[i], recv_sem=rsem.at[i],
            device_id=device, device_id_type=pl.DeviceIdType.MESH,
        )
        copy.start()
        started.append(copy)
        return copy

    barrier = pltpu.get_barrier_semaphore()
    peers = [at_z(k) for k in far_z] + [at_p(k) for k in far_p] + [partner]
    for peer in peers:
        pl.semaphore_signal(barrier, inc=1, device_id=peer, device_id_type=pl.DeviceIdType.MESH)

    ca, cc, cac, cb = pl.ds(0, NA), pl.ds(NA, NC), pl.ds(0, wide), pl.ds(wide, NB)
    own_rows = (
        pltpu.make_async_copy(hid_hbm.at[0, :, cac], zb.at[z], lsem.at[10]),
        pltpu.make_async_copy(hid_hbm.at[0, :, cb], pb.at[section], lsem.at[11]),
    )
    for load in own_rows:
        load.start()

    loads = [pltpu.make_async_copy(w_hbm, w, lsem.at[0]), pltpu.make_async_copy(len_hbm, lengths, lsem.at[9])]
    for k in range(8):
        loads.append(pltpu.make_async_copy(tl_hbm.at[:, pl.ds(8 * k, 8), :], tl.at[k], lsem.at[k + 1]))
    for load in loads:
        load.start()
    for load in own_rows:
        load.wait()
    pl.semaphore_wait(barrier, len(peers))

    zs = [send(zb.at[z], zb.at[z], at_z(k)) for k in far_z]
    ps = [send(pb.at[section], pb.at[section], at_p(k)) for k in far_p]
    acc[...] = jnp.zeros_like(acc)
    loads[1].wait()

    def position(r, j):
        e1 = lengths[0, r]
        e2 = e1 + lengths[1, r]
        e3 = e2 + lengths[2, r]
        late = jnp.where(j >= e3, 3 * SEQ_MB - e3, 2 * SEQ_MB - e2)
        early = jnp.where(j >= e1, SEQ_MB - e1, 0)
        return j + jnp.where(j >= e2, late, early)

    def picked(r, rows):
        j = lax.broadcasted_iota(jnp.int32, (LIVE, 128), 0)
        p = lax.broadcasted_iota(jnp.int32, (LIVE, 128), 1)
        pick = (p == position(r, j)).astype(F32).astype(BF16)
        return jnp.dot(pick, rows, preferred_element_type=F32).astype(BF16)

    def put_back(r, rows):
        p = lax.broadcasted_iota(jnp.int32, (128, LIVE), 0)
        j = lax.broadcasted_iota(jnp.int32, (128, LIVE), 1)
        place = (p == position(r, j)).astype(F32).astype(BF16)
        return jnp.dot(place, rows, preferred_element_type=F32)

    for copy in zs:
        copy.wait_recv()
    hb[x, y] = zb[...].astype(F32).reshape(NZ * 8, wide).astype(BF16)

    def a_at(xx, k):
        return hb.at[(x + xx) % NX, (y + k) % NY, :, ca]

    def c_at(yy, k):
        return hb.at[(x + k) % NX, (y + yy) % NY, :, cc]

    blocks = (a_at, c_at)
    along = (at_x, at_y)
    across = (at_y, at_x)

    def odd(part, k):
        return ((y, x)[part] + k) % 2

    spread, near, passed = {}, {}, {}

    def send_near(part, k):
        block = blocks[part](0, k)
        near[part, k] = (send(block, block, along[part](1)), send(block, block, along[part](3)))

    def pass_on(part, k):
        for copy in near[part, k]:
            copy.wait_recv()
        back = 2 * odd(part, k)
        block = blocks[part](3 + back, k)
        passed[part, k] = send(block, block, along[part](1 + back))

    for k in (2, 1, 3):
        for part in range(2):
            block = blocks[part](0, 0)
            spread[part, k] = send(block, block, across[part](k))
    for part in range(2):
        send_near(part, 0)
    for copy in ps:
        copy.wait_recv()
    hz[z] = picked(z, pb[...].astype(F32).reshape(128, NB).astype(BF16))

    def b_pass(step, right):
        i = (z - step) % NZ if right else (z + step) % NZ
        part = hz.at[i] if step < 3 else hz.at[i, :, pl.ds(0 if right else HB, HB)]
        return send(part, part, at_z(1 if right else NZ - 1))

    ring = [(b_pass(0, True), b_pass(0, False))]

    def b_forward(step):
        ring[step - 1][0].wait_recv()
        right = b_pass(step, True)
        ring[step - 1][1].wait_recv()
        ring.append((right, b_pass(step, False)))

    for k in (1, 3):
        for part in range(2):
            spread[part, k].wait_recv()
            send_near(part, 4 - k)
    b_forward(1)
    for part in range(2):
        spread[part, 2].wait_recv()
        send_near(part, 2)
    for part in range(2):
        pass_on(part, 0)
    def a_logits(i):
        rows = hb[i, :, :, 0:NA].reshape(256, NA)
        block = jnp.dot(rows, w[0:NA], preferred_element_type=F32)
        acc[i] = acc[i] + block.reshape(4, 8, 8, vocab)

    def c_logits(i):
        rows = hb[:, i, :, NA:wide].reshape(256, NC)
        block = jnp.dot(rows, w[NA:wide], preferred_element_type=F32)
        acc[:, i] = acc[:, i] + block.reshape(4, 8, 8, vocab)

    def b_logits(i):
        rows = put_back(i, hz[i]).astype(BF16)
        block = jnp.dot(rows, w[wide:], preferred_element_type=F32)
        acc[:, :, i] = acc[:, :, i] + block.reshape(4, 4, 8, vocab)

    def c_far(owner):
        rows = hb[pl.ds(2 * owner, 2), (y + 2) % NY, :, NA:wide].reshape(128, NC)
        block = jnp.dot(rows, w[NA:wide], preferred_element_type=F32)
        into = acc.at[pl.ds(2 * owner, 2), (y + 2) % NY]
        into[...] = into[...] + block.reshape(2, 8, 8, vocab)

    for load in [loads[0]] + loads[2:]:
        load.wait()

    def teacher_block(k, carry):
        tp[k] = jnp.exp(tl[k])
        return carry

    lax.fori_loop(0, 8, teacher_block, 0)
    b_logits(z)
    a_logits(x)
    c_logits(y)
    for k in (1, 3):
        for part in range(2):
            pass_on(part, k)
    b_forward(2)
    b_logits((z + 1) % NZ)
    b_logits((z + 7) % NZ)
    for part in range(2):
        pass_on(part, 2)
    for k in (1, 3):
        a_logits((x + k) % NX)
        c_logits((y + k) % NY)
    b_forward(3)
    b_logits((z + 2) % NZ)
    b_logits((z + 6) % NZ)
    b_logits((z + 3) % NZ)
    b_logits((z + 5) % NZ)
    for k in range(4):
        passed[0, k].wait_recv()
    a_logits((x + 2) % NX)
    for k in range(4):
        passed[1, k].wait_recv()
    for copy in ring[3]:
        copy.wait_recv()
    b_logits((z + 4) % NZ)
    c_far(other)
    exchanges = []
    for k in range(4):
        block = acc.at[2 * other + k // 2, pl.ds(2 * (k % 2), 2)]
        exchanges.append(send(block, lrecv.at[pl.ds(2 * k, 2)], partner))
    c_far(t)

    row_i = lax.broadcasted_iota(jnp.int32, (128, 128), 0)
    lane_i = lax.broadcasted_iota(jnp.int32, (128, 128), 1)
    eye = row_i == lane_i

    def to_lanes(col):
        return jnp.sum(jnp.where(eye, col, 0.0), axis=0, keepdims=True)

    def to_rows(lane):
        return jnp.sum(jnp.where(eye, lane, 0.0), axis=1, keepdims=True)

    for k in range(4):
        exchanges[k].wait_recv()
        pair = slice(2 * k, 2 * k + 2)
        both = acc[2 * t + k // 2, 2 * (k % 2):2 * (k % 2) + 2] + lrecv[pair]
        lrecv[pair] = both
        logits = both.reshape(128, vocab)
        teacher = tl[pair].reshape(128, vocab)
        prob = tp[pair].reshape(128, vocab)
        top = jnp.max(logits, axis=1, keepdims=True)
        total = jnp.sum(jnp.exp(logits - top), axis=1, keepdims=True)
        cross = jnp.sum(prob * (teacher - logits), axis=1, keepdims=True)
        mass = jnp.sum(prob, axis=1, keepdims=True)
        stats[0, k:k + 1, :] = to_lanes(top)
        stats[0, 4 + k:5 + k, :] = to_lanes(total)
        stats[0, 8 + k:9 + k, :] = to_lanes(cross)
        stats[0, 12 + k:13 + k, :] = to_lanes(mass)

    for level, (slots, at, order) in enumerate(((rz, at_z, far_z), (rp, at_p, far_p))):
        copies = [send(stats.at[level], slots.at[k - 1], at(k)) for k in order]
        for copy in copies:
            copy.wait_recv()
        parts = [stats[level]] + [slots[k] for k in range(len(order))]
        top = parts[0][0:4]
        for part in parts[1:]:
            top = jnp.maximum(top, part[0:4])
        total = sum(part[4:8] * jnp.exp(part[0:4] - top) for part in parts)
        sums = sum(part[8:16] for part in parts)
        stats[level + 1, 0:4, :] = top
        stats[level + 1, 4:8, :] = total
        stats[level + 1, 8:16, :] = sums

    log_norm = stats[2, 0:4, :] + jnp.log(stats[2, 4:8, :])
    cross, mass = stats[2, 8:12, :], stats[2, 12:16, :]
    row_id = lax.broadcasted_iota(jnp.int32, (4, 128), 0) * 128 + lax.broadcasted_iota(jnp.int32, (4, 128), 1)
    local_section, replica, inner = row_id // 64, (row_id // 8) % 8, row_id % 8
    within = (local_section % 4) * 8 + inner
    micro = local_section // 4
    chosen = jnp.ones((4, 128), jnp.int32)
    for r in range(NZ):
        for m in range(2):
            length = jnp.where(t == 0, lengths[m, r], lengths[m + 2, r])
            chosen = jnp.where((replica == r) & (micro == m), length, chosen)
    live = (within < chosen).astype(F32)
    weight = live * (SEQ_MB / chosen.astype(F32))
    divergence = live * (cross + log_norm * mass)
    scale = weight * mass

    div_total = jnp.zeros((1, 128), F32)
    swaps = []
    for k in range(4):
        norm_rows = to_rows(log_norm[k:k + 1])
        scale_rows = to_rows(scale[k:k + 1])
        weight_rows = to_rows(weight[k:k + 1])
        pair = slice(2 * k, 2 * k + 2)
        logits = lrecv[pair].reshape(128, vocab)
        prob = tp[pair].reshape(128, vocab)
        grad = jnp.exp(logits - norm_rows) * scale_rows - weight_rows * prob
        g[2 * t + k // 2, 2 * (k % 2):2 * (k % 2) + 2] = grad.reshape(2, 8, 8, vocab).astype(BF16)
        mine = g.at[2 * t + k // 2, pl.ds(2 * (k % 2), 2)]
        swaps.append(send(mine, mine, partner))
    for k in range(4):
        div_rows = to_rows(divergence[k:k + 1])
        place = (2 * k + row_i // 64) * 8 + row_i % 8
        pick = (lane_i == place) & ((row_i // 8) % 8 == z)
        div_total = div_total + jnp.sum(jnp.where(pick, div_rows, 0.0), axis=0, keepdims=True)
    div_ref[...] = div_total[:, 0:64]
    for copy in swaps:
        copy.wait_recv()

    def times_w(rows, start, size):
        return lax.dot_general(
            rows, w[start:start + size, :], (((1,), (1,)), ((), ())), preferred_element_type=F32
        )

    def product(part, o):
        rows = g[(x + o) % NX] if part == 0 else g[:, (y + o) % NY]
        rows = rows.astype(F32).reshape(256, vocab).astype(BF16)
        return times_w(rows, (0, NA)[part], size[part]).reshape(4, 64, size[part])

    def b_product(o):
        i = (z + o) % NZ
        rows = g[:, :, i].astype(F32).reshape(128, vocab).astype(BF16)
        prod[i] = times_w(picked(i, rows), wide, NB)

    size = (NA, NC)
    fit = (pl.ds(0, NA), pl.ds(0, NC))
    mine = (y, x)
    order = (2, 1, 3, 0)
    halves = (slice(0, HB), slice(HB, NB))

    def b_item(side, item, extra=None):
        step = 0 if item == 0 else (item + 1) // 2
        upper = (item % 2 == 0) if side == 0 else (item % 2 == 1)
        owner = (z + 4 - step) % NZ if side == 0 else (z + 4 + step) % NZ
        value = prod[owner, :, halves[0 if upper else 1]]
        if extra is not None:
            value = value + extra
        sb[side, item] = value.astype(BF16)
        return send(sb.at[side, item], rb.at[side, item], at_z(1 if side == 0 else NZ - 1))

    hop, direct = {}, {}
    b_product(4)
    sides = [[b_item(side, 0)] for side in range(2)]
    for part in range(2):
        s1[part, :, :, fit[part]] = product(part, 2).astype(BF16)
        for k in order:
            back = 2 * odd(part, k)
            hop[part, k] = send(
                s1.at[part, (mine[part] + k) % 4, :, fit[part]], r1h.at[part, k, :, fit[part]], along[part](1 + back)
            )
    for side in range(2):
        b_product((3, 5)[side])
        sides[side].append(b_item(side, 1))

    def b_next(item):
        source = 0 if item == 2 else item - 2
        for side in range(2):
            sides[side][source].wait_recv()
            sides[side].append(b_item(side, item, rb[side, source].astype(F32)))

    for part in range(2):
        f1[part, 0, :, :, fit[part]] = product(part, 1)
        f1[part, 1, :, :, fit[part]] = product(part, 3)
        for k in order:
            back = odd(part, k)
            sd[part, 0, k, :, fit[part]] = f1[part, 1 - back, (mine[part] + k) % 4, :, fit[part]].astype(BF16)
            direct[part, 0, k] = send(
                sd.at[part, 0, k, :, fit[part]], r1f.at[part, 0, k, :, fit[part]], along[part](3 - 2 * back)
            )
    b_next(2)
    b_product(2)
    b_product(6)
    for k in order:
        for part in range(2):
            hop[part, k].wait_recv()
            back = odd(part, k)
            value = f1[part, back, (mine[part] + k) % 4, :, fit[part]] + r1h[part, k, :, fit[part]].astype(F32)
            sd[part, 1, k, :, fit[part]] = value.astype(BF16)
            direct[part, 1, k] = send(
                sd.at[part, 1, k, :, fit[part]], r1f.at[part, 1, k, :, fit[part]], along[part](1 + 2 * back)
            )
    b_next(3)
    b_product(1)
    b_product(7)
    b_product(0)
    for part in range(2):
        own1[part, :, :, fit[part]] = product(part, 0)
    b_next(4)

    def whole(part, k):
        direct[part, 0, k].wait_recv()
        direct[part, 1, k].wait_recv()
        value = own1[part, (mine[part] + k) % 4, :, fit[part]]
        return value + r1f[part, 0, k, :, fit[part]].astype(F32) + r1f[part, 1, k, :, fit[part]].astype(F32)

    ph2 = []

    def second(k):
        for part in range(2):
            s2[part, k - 1, :, fit[part]] = whole(part, k).astype(BF16)
            ph2.append(send(
                s2.at[part, k - 1, :, fit[part]], r2.at[part, k - 1, :, fit[part]], across[part](k)
            ))

    second(2)
    b_next(5)
    second(1)
    second(3)
    for part in range(2):
        own1[part, mine[part], :, fit[part]] = whole(part, 0)
    b_next(6)
    for copy in ph2:
        copy.wait_recv()
    for part in range(2):
        value = own1[part, mine[part], :, fit[part]]
        for k in range(3):
            value = value + r2[part, k, :, fit[part]].astype(F32)
        start = (0, NA)[part]
        u[:, :, start:start + size[part]] = value.reshape(NZ, 8, size[part])
    s3[...] = u[...].astype(BF16)
    zs = [send(s3.at[(z + k) % NZ], r3.at[k - 1], at_z(k)) for k in far_z]
    for side in range(2):
        for item in (5, 6):
            sides[side][item].wait_recv()
    b_first = prod[z, :, halves[0]] + rb[0, 6].astype(F32) + rb[1, 5].astype(F32)
    b_second = prod[z, :, halves[1]] + rb[0, 5].astype(F32) + rb[1, 6].astype(F32)
    live_rows = jnp.concatenate([b_first.astype(BF16), b_second.astype(BF16)], axis=1)
    s4[...] = put_back(z, live_rows).reshape(16, 8, NB).astype(BF16)
    ps = [send(s4.at[plane(k)], r4.at[k - 1], at_p(k)) for k in far_p]
    for copy in zs:
        copy.wait_recv()
    total = u[z]
    for k in range(NZ - 1):
        total = total + r3[k].astype(F32)
    grad_ref[0, :, 0:wide] = total.astype(BF16)
    for copy in ps:
        copy.wait_recv()
    total = s4[section].astype(F32)
    for k in range(15):
        total = total + r4[k].astype(F32)
    grad_ref[0, :, wide:] = total.astype(BF16)

    for copy in started:
        copy.wait_send()


def hand_over(grad_ref, div_ref, grad_out, div_out):
    grad_out[...] = grad_ref[...]
    div_out[...] = div_ref[...]


N_SEM = 176


def body(hidden, head_weight, teacher_logprobs, lengths):
    width, vocab = head_weight.shape
    wide = NA + NC
    V = pltpu.VMEM
    scratch = [
        V((width, vocab), BF16),
        V((8, 8, 8, vocab), F32),
        V((8, 8, 8, vocab), F32),
        pltpu.SMEM((4, 8), jnp.int32),
        V((NZ, 8, wide), BF16),
        V((16, 8, NB), BF16),
        V((NX, NY, 64, wide), BF16),
        V((NZ, LIVE, NB), BF16),
        V((NX, NY, 8, 8, vocab), F32),
        V((8, 8, 8, vocab), F32),
        V((3, 16, 128), F32),
        V((NZ - 1, 16, 128), F32),
        V((15, 16, 128), F32),
        V((NX, NY, 8, 8, vocab), BF16),
        V((2, 4, 64, NA), BF16),
        V((2, 2, 4, 64, NA), F32),
        V((2, 4, 64, NA), F32),
        V((2, 4, 64, NA), BF16),
        V((2, 2, 4, 64, NA), BF16),
        V((2, 2, 4, 64, NA), BF16),
        V((2, 3, 64, NA), BF16),
        V((2, 3, 64, NA), BF16),
        V((NZ, 8, wide), F32),
        V((NZ, 8, wide), BF16),
        V((NZ - 1, 8, wide), BF16),
        V((NZ, LIVE, NB), F32),
        V((2, 7, LIVE, HB), BF16),
        V((2, 7, LIVE, HB), BF16),
        V((16, 8, NB), BF16),
        V((15, 8, NB), BF16),
        pltpu.SemaphoreType.DMA((12,)),
        pltpu.SemaphoreType.DMA((N_SEM,)),
        pltpu.SemaphoreType.DMA((N_SEM,)),
    ]
    grad, divergence = pl.pallas_call(
        kernel,
        out_shape=(
            jax.ShapeDtypeStruct((1, 8, width), BF16),
            jax.ShapeDtypeStruct((1, 64), F32),
        ),
        in_specs=[
            pl.BlockSpec(memory_space=pl.ANY),
            pl.BlockSpec(memory_space=pl.ANY),
            pl.BlockSpec(memory_space=pl.ANY),
            pl.BlockSpec(memory_space=pl.ANY),
        ],
        out_specs=(pl.BlockSpec(memory_space=V), pl.BlockSpec(memory_space=V)),
        scratch_shapes=scratch,
        compiler_params=pltpu.CompilerParams(
            collective_id=0, has_side_effects=True, vmem_limit_bytes=56 * 1024 * 1024
        ),
        name="distill",
    )(hidden, head_weight, teacher_logprobs, lengths.T)
    return pl.pallas_call(
        hand_over,
        out_shape=(
            jax.ShapeDtypeStruct(grad.shape, grad.dtype),
            jax.ShapeDtypeStruct(divergence.shape, divergence.dtype),
        ),
        in_specs=[pl.BlockSpec(memory_space=V)] * 2,
        out_specs=(pl.BlockSpec(memory_space=V), pl.BlockSpec(memory_space=V)),
        name="hand_over",
    )(grad, divergence)


def solution(mesh):
    placed = (
        P("dp", "section", "tensor"),
        P("tensor", ("section", "dp")),
        P(None, "tensor", ("section", "dp")),
        P(),
    )
    return jax.shard_map(
        body,
        mesh=mesh,
        in_specs=placed,
        out_specs=(P("dp", "section", "tensor"), P("dp", "tensor")),
        check_vma=False,
    )
```

```python
import jax
import jax.numpy as jnp
from jax import lax
from jax.experimental import pallas as pl
from jax.experimental.pallas import tpu as pltpu
from jax.sharding import PartitionSpec as P

SEQ_MB, LIVE = 32, 80
NX, NY, NZ = 4, 4, 8
NA, NB = 512, 768
HB = NB // 2
F32, BF16 = jnp.float32, jnp.bfloat16


def kernel(
    hid_hbm, w_hbm, tl_hbm, len_hbm, grad_ref, div_ref,
    w, tl, tp, lengths, zb, pb, hb, hz, acc, lrecv, stats, rz, rp, g,
    s1, f1, own1, r1h, r1f, s2, r2, u, s3, r3, prod, sb, rb, s4, r4,
    lsem, ssem, rsem,
):
    wide = NA + NA
    vocab = w.shape[1]
    section, z, t = lax.axis_index("section"), lax.axis_index("dp"), lax.axis_index("tensor")
    x, y = section // NY, section % NY
    other = 1 - t

    def at_x(k):
        return (((x + k) % NX) * NY + y, z, t)

    def at_y(k):
        return (x * NY + (y + k) % NY, z, t)

    def at_z(k):
        return (section, (z + k) % NZ, t)

    def plane(k):
        return ((x + k // NY) % NX) * NY + (y + k % NY) % NY

    def at_p(k):
        return (plane(k), z, t)

    far_z = (4, 3, 5, 2, 6, 1, 7)
    far_p = (10, 6, 14, 9, 11, 2, 8, 5, 7, 13, 15, 1, 3, 4, 12)
    partner = (section, z, other)
    started = []

    def send(src, dst, device):
        i = len(started)
        copy = pltpu.make_async_remote_copy(
            src_ref=src, dst_ref=dst, send_sem=ssem.at[i], recv_sem=rsem.at[i],
            device_id=device, device_id_type=pl.DeviceIdType.MESH,
        )
        copy.start()
        started.append(copy)
        return copy

    barrier = pltpu.get_barrier_semaphore()
    peers = [at_z(k) for k in far_z] + [at_p(k) for k in far_p] + [partner]
    for peer in peers:
        pl.semaphore_signal(barrier, inc=1, device_id=peer, device_id_type=pl.DeviceIdType.MESH)

    ca, cc, cac, cb = pl.ds(0, NA), pl.ds(NA, NA), pl.ds(0, wide), pl.ds(wide, NB)
    own_rows = (
        pltpu.make_async_copy(hid_hbm.at[0, :, cac], zb.at[z], lsem.at[10]),
        pltpu.make_async_copy(hid_hbm.at[0, :, cb], pb.at[section], lsem.at[11]),
    )
    for load in own_rows:
        load.start()

    loads = [pltpu.make_async_copy(w_hbm, w, lsem.at[0]), pltpu.make_async_copy(len_hbm, lengths, lsem.at[9])]
    for k in range(8):
        loads.append(pltpu.make_async_copy(tl_hbm.at[:, pl.ds(8 * k, 8), :], tl.at[k], lsem.at[k + 1]))
    for load in loads:
        load.start()
    for load in own_rows:
        load.wait()
    pl.semaphore_wait(barrier, len(peers))

    zs = [send(zb.at[z], zb.at[z], at_z(k)) for k in far_z]
    ps = [send(pb.at[section], pb.at[section], at_p(k)) for k in far_p]
    acc[...] = jnp.zeros_like(acc)
    loads[1].wait()

    def position(r, j):
        e1 = lengths[0, r]
        e2 = e1 + lengths[1, r]
        e3 = e2 + lengths[2, r]
        late = jnp.where(j >= e3, 3 * SEQ_MB - e3, 2 * SEQ_MB - e2)
        early = jnp.where(j >= e1, SEQ_MB - e1, 0)
        return j + jnp.where(j >= e2, late, early)

    def picked(r, rows):
        j = lax.broadcasted_iota(jnp.int32, (LIVE, 128), 0)
        p = lax.broadcasted_iota(jnp.int32, (LIVE, 128), 1)
        pick = (p == position(r, j)).astype(F32).astype(BF16)
        return jnp.dot(pick, rows, preferred_element_type=F32).astype(BF16)

    def put_back(r, rows):
        p = lax.broadcasted_iota(jnp.int32, (128, LIVE), 0)
        j = lax.broadcasted_iota(jnp.int32, (128, LIVE), 1)
        place = (p == position(r, j)).astype(F32).astype(BF16)
        return jnp.dot(place, rows, preferred_element_type=F32)

    for copy in zs:
        copy.wait_recv()
    hb[x, y] = zb[...].astype(F32).reshape(NZ * 8, wide).astype(BF16)
    ph2 = []
    for k in (2, 1, 3):
        ph2.append(send(hb.at[x, y, :, ca], hb.at[x, y, :, ca], at_y(k)))
        ph2.append(send(hb.at[x, y, :, cc], hb.at[x, y, :, cc], at_x(k)))
    for copy in ps:
        copy.wait_recv()
    hz[z] = picked(z, pb[...].astype(F32).reshape(128, NB).astype(BF16))

    def b_pass(step, right):
        i = (z - step) % NZ if right else (z + step) % NZ
        part = hz.at[i] if step < 3 else hz.at[i, :, pl.ds(0 if right else HB, HB)]
        return send(part, part, at_z(1 if right else NZ - 1))

    ring = [(b_pass(0, True), b_pass(0, False))]

    def b_forward(step):
        ring[step - 1][0].wait_recv()
        right = b_pass(step, True)
        ring[step - 1][1].wait_recv()
        ring.append((right, b_pass(step, False)))

    b_forward(1)

    for copy in ph2:
        copy.wait_recv()
    y1, y3, x1, x3 = (y + 1) % NY, (y + 3) % NY, (x + 1) % NX, (x + 3) % NX
    lo2, hi2 = pl.ds(0, 2), pl.ds(2, 2)

    def a_block(i, part):
        return hb.at[i, part, :, ca]

    def c_block(i, part):
        return hb.at[part, i, :, cc]

    ar0 = send(a_block(x, lo2), a_block(x, lo2), at_x(1))
    br0 = send(c_block(y, lo2), c_block(y, lo2), at_y(1))
    al0 = send(a_block(x, hi2), a_block(x, hi2), at_x(3))
    bl0 = send(c_block(y, hi2), c_block(y, hi2), at_y(3))
    ar1 = send(a_block(x, hi2), a_block(x, hi2), at_x(1))
    br1 = send(c_block(y, hi2), c_block(y, hi2), at_y(1))
    al1 = send(a_block(x, lo2), a_block(x, lo2), at_x(3))
    bl1 = send(c_block(y, lo2), c_block(y, lo2), at_y(3))

    def a_logits(i):
        rows = hb[i, :, :, 0:NA].reshape(256, NA)
        block = jnp.dot(rows, w[0:NA], preferred_element_type=F32)
        acc[i] = acc[i] + block.reshape(4, 8, 8, vocab)

    def c_logits(i):
        rows = hb[:, i, :, NA:wide].reshape(256, NA)
        block = jnp.dot(rows, w[NA:wide], preferred_element_type=F32)
        acc[:, i] = acc[:, i] + block.reshape(4, 8, 8, vocab)

    def b_logits(i):
        rows = put_back(i, hz[i]).astype(BF16)
        block = jnp.dot(rows, w[wide:], preferred_element_type=F32)
        acc[:, :, i] = acc[:, :, i] + block.reshape(4, 4, 8, vocab)

    def c_far(owner):
        rows = hb[pl.ds(2 * owner, 2), (y + 2) % NY, :, NA:wide].reshape(128, NA)
        block = jnp.dot(rows, w[NA:wide], preferred_element_type=F32)
        into = acc.at[pl.ds(2 * owner, 2), (y + 2) % NY]
        into[...] = into[...] + block.reshape(2, 8, 8, vocab)

    for load in [loads[0]] + loads[2:]:
        load.wait()

    def teacher_block(k, carry):
        tp[k] = jnp.exp(tl[k])
        return carry

    lax.fori_loop(0, 8, teacher_block, 0)
    b_logits(z)
    a_logits(x)
    c_logits(y)

    b_forward(2)
    b_logits((z + 1) % NZ)
    b_logits((z + 7) % NZ)
    ar0.wait_recv()
    ar2 = send(a_block(x3, lo2), a_block(x3, lo2), at_x(1))
    br0.wait_recv()
    br2 = send(c_block(y3, lo2), c_block(y3, lo2), at_y(1))
    al0.wait_recv()
    al2 = send(a_block(x1, hi2), a_block(x1, hi2), at_x(3))
    bl0.wait_recv()
    bl2 = send(c_block(y1, hi2), c_block(y1, hi2), at_y(3))
    b_forward(3)
    b_logits((z + 2) % NZ)
    b_logits((z + 6) % NZ)
    for copy in [ar1, br1, al1, bl1]:
        copy.wait_recv()
    for k in (1, 3):
        a_logits((x + k) % NX)
        c_logits((y + k) % NY)
    b_logits((z + 3) % NZ)
    b_logits((z + 5) % NZ)
    for copy in ring[3]:
        copy.wait_recv()
    b_logits((z + 4) % NZ)
    for copy in (ar2, al2):
        copy.wait_recv()
    a_logits((x + 2) % NX)
    for copy in (br2, bl2):
        copy.wait_recv()
    c_far(other)
    exchanges = []
    for k in range(4):
        block = acc.at[2 * other + k // 2, pl.ds(2 * (k % 2), 2)]
        exchanges.append(send(block, lrecv.at[pl.ds(2 * k, 2)], partner))
    c_far(t)

    row_i = lax.broadcasted_iota(jnp.int32, (128, 128), 0)
    lane_i = lax.broadcasted_iota(jnp.int32, (128, 128), 1)
    eye = row_i == lane_i

    def to_lanes(col):
        return jnp.sum(jnp.where(eye, col, 0.0), axis=0, keepdims=True)

    def to_rows(lane):
        return jnp.sum(jnp.where(eye, lane, 0.0), axis=1, keepdims=True)

    for k in range(4):
        exchanges[k].wait_recv()
        pair = slice(2 * k, 2 * k + 2)
        both = acc[2 * t + k // 2, 2 * (k % 2):2 * (k % 2) + 2] + lrecv[pair]
        lrecv[pair] = both
        logits = both.reshape(128, vocab)
        teacher = tl[pair].reshape(128, vocab)
        prob = tp[pair].reshape(128, vocab)
        top = jnp.max(logits, axis=1, keepdims=True)
        total = jnp.sum(jnp.exp(logits - top), axis=1, keepdims=True)
        cross = jnp.sum(prob * (teacher - logits), axis=1, keepdims=True)
        mass = jnp.sum(prob, axis=1, keepdims=True)
        stats[0, k:k + 1, :] = to_lanes(top)
        stats[0, 4 + k:5 + k, :] = to_lanes(total)
        stats[0, 8 + k:9 + k, :] = to_lanes(cross)
        stats[0, 12 + k:13 + k, :] = to_lanes(mass)

    for level, (slots, at, order) in enumerate(((rz, at_z, far_z), (rp, at_p, far_p))):
        copies = [send(stats.at[level], slots.at[k - 1], at(k)) for k in order]
        for copy in copies:
            copy.wait_recv()
        parts = [stats[level]] + [slots[k] for k in range(len(order))]
        top = parts[0][0:4]
        for part in parts[1:]:
            top = jnp.maximum(top, part[0:4])
        total = sum(part[4:8] * jnp.exp(part[0:4] - top) for part in parts)
        sums = sum(part[8:16] for part in parts)
        stats[level + 1, 0:4, :] = top
        stats[level + 1, 4:8, :] = total
        stats[level + 1, 8:16, :] = sums

    log_norm = stats[2, 0:4, :] + jnp.log(stats[2, 4:8, :])
    cross, mass = stats[2, 8:12, :], stats[2, 12:16, :]
    row_id = lax.broadcasted_iota(jnp.int32, (4, 128), 0) * 128 + lax.broadcasted_iota(jnp.int32, (4, 128), 1)
    local_section, replica, inner = row_id // 64, (row_id // 8) % 8, row_id % 8
    within = (local_section % 4) * 8 + inner
    micro = local_section // 4
    chosen = jnp.ones((4, 128), jnp.int32)
    for r in range(NZ):
        for m in range(2):
            length = jnp.where(t == 0, lengths[m, r], lengths[m + 2, r])
            chosen = jnp.where((replica == r) & (micro == m), length, chosen)
    live = (within < chosen).astype(F32)
    weight = live * (SEQ_MB / chosen.astype(F32))
    divergence = live * (cross + log_norm * mass)
    scale = weight * mass

    div_total = jnp.zeros((1, 128), F32)
    swaps = []
    for k in range(4):
        norm_rows = to_rows(log_norm[k:k + 1])
        scale_rows = to_rows(scale[k:k + 1])
        weight_rows = to_rows(weight[k:k + 1])
        pair = slice(2 * k, 2 * k + 2)
        logits = lrecv[pair].reshape(128, vocab)
        prob = tp[pair].reshape(128, vocab)
        grad = jnp.exp(logits - norm_rows) * scale_rows - weight_rows * prob
        g[2 * t + k // 2, 2 * (k % 2):2 * (k % 2) + 2] = grad.reshape(2, 8, 8, vocab).astype(BF16)
        mine = g.at[2 * t + k // 2, pl.ds(2 * (k % 2), 2)]
        swaps.append(send(mine, mine, partner))
    for k in range(4):
        div_rows = to_rows(divergence[k:k + 1])
        place = (2 * k + row_i // 64) * 8 + row_i % 8
        pick = (lane_i == place) & ((row_i // 8) % 8 == z)
        div_total = div_total + jnp.sum(jnp.where(pick, div_rows, 0.0), axis=0, keepdims=True)
    div_ref[...] = div_total[:, 0:64]
    for copy in swaps:
        copy.wait_recv()

    def times_w(rows, start, size):
        return lax.dot_general(
            rows, w[start:start + size, :], (((1,), (1,)), ((), ())), preferred_element_type=F32
        )

    def product(part, o):
        rows = g[(x + o) % NX] if part == 0 else g[:, (y + o) % NY]
        rows = rows.astype(F32).reshape(256, vocab).astype(BF16)
        return times_w(rows, part * NA, NA).reshape(4, 64, NA)

    def b_product(o):
        i = (z + o) % NZ
        rows = g[:, :, i].astype(F32).reshape(128, vocab).astype(BF16)
        prod[i] = times_w(picked(i, rows), wide, NB)

    first = (at_x, at_y)
    second = (at_y, at_x)
    halves = (slice(0, HB), slice(HB, NB))

    def b_item(side, item, extra=None):
        step = 0 if item == 0 else (item + 1) // 2
        upper = (item % 2 == 0) if side == 0 else (item % 2 == 1)
        owner = (z + 4 - step) % NZ if side == 0 else (z + 4 + step) % NZ
        value = prod[owner, :, halves[0 if upper else 1]]
        if extra is not None:
            value = value + extra
        sb[side, item] = value.astype(BF16)
        return send(sb.at[side, item], rb.at[side, item], at_z(1 if side == 0 else NZ - 1))

    hop, direct = [], []
    for part in range(2):
        s1[part, 2] = product(part, 2).astype(BF16)
        hop.append((
            send(s1.at[part, 2, lo2], r1h.at[part, 0], first[part](1)),
            send(s1.at[part, 2, hi2], r1h.at[part, 1], first[part](3)),
        ))
    b_product(4)
    sides = [[b_item(side, 0)] for side in range(2)]
    def b_next(item):
        source = 0 if item == 2 else item - 2
        for side in range(2):
            sides[side][source].wait_recv()
            sides[side].append(b_item(side, item, rb[side, source].astype(F32)))

    for part in range(2):
        block = product(part, 1)
        f1[part, 0] = block[0:2]
        s1[part, 1, 2:4] = block[2:4].astype(BF16)
        direct.append(send(s1.at[part, 1, hi2], r1f.at[part, 0, hi2], first[part](1)))
        block = product(part, 3)
        f1[part, 1] = block[2:4]
        s1[part, 3, 0:2] = block[0:2].astype(BF16)
        direct.append(send(s1.at[part, 3, lo2], r1f.at[part, 1, lo2], first[part](3)))
    for side in range(2):
        b_product((3, 5)[side])
        sides[side].append(b_item(side, 1))
    b_next(2)
    b_product(2)
    b_product(6)
    for part in range(2):
        hop[part][0].wait_recv()
        s1[part, 1, 0:2] = (f1[part, 0] + r1h[part, 0].astype(F32)).astype(BF16)
        direct.append(send(s1.at[part, 1, lo2], r1f.at[part, 0, lo2], first[part](1)))
        hop[part][1].wait_recv()
        s1[part, 3, 2:4] = (f1[part, 1] + r1h[part, 1].astype(F32)).astype(BF16)
        direct.append(send(s1.at[part, 3, hi2], r1f.at[part, 1, hi2], first[part](3)))
    b_next(3)
    b_product(1)
    b_product(7)
    b_product(0)
    for part in range(2):
        own1[part] = product(part, 0)
    b_next(4)
    b_next(5)
    for copy in direct:
        copy.wait_recv()
    place2 = (y, x)
    ph2 = []
    for k in (2, 1, 3):
        for part in range(2):
            i = (place2[part] + k) % 4
            value = own1[part, i] + r1f[part, 0, i].astype(F32) + r1f[part, 1, i].astype(F32)
            s2[part, k - 1] = value.astype(BF16)
            ph2.append(send(s2.at[part, k - 1], r2.at[part, k - 1], second[part](k)))
    b_next(6)
    for copy in ph2:
        copy.wait_recv()
    for part in range(2):
        i = place2[part]
        value = own1[part, i] + r1f[part, 0, i].astype(F32) + r1f[part, 1, i].astype(F32)
        for k in range(3):
            value = value + r2[part, k].astype(F32)
        u[:, :, part * NA:(part + 1) * NA] = value.reshape(NZ, 8, NA)
    s3[...] = u[...].astype(BF16)
    zs = [send(s3.at[(z + k) % NZ], r3.at[k - 1], at_z(k)) for k in far_z]
    for side in range(2):
        for item in (5, 6):
            sides[side][item].wait_recv()
    b_first = prod[z, :, halves[0]] + rb[0, 6].astype(F32) + rb[1, 5].astype(F32)
    b_second = prod[z, :, halves[1]] + rb[0, 5].astype(F32) + rb[1, 6].astype(F32)
    live_rows = jnp.concatenate([b_first.astype(BF16), b_second.astype(BF16)], axis=1)
    s4[...] = put_back(z, live_rows).reshape(16, 8, NB).astype(BF16)
    ps = [send(s4.at[plane(k)], r4.at[k - 1], at_p(k)) for k in far_p]
    for copy in zs:
        copy.wait_recv()
    total = u[z]
    for k in range(NZ - 1):
        total = total + r3[k].astype(F32)
    grad_ref[0, :, 0:wide] = total.astype(BF16)
    for copy in ps:
        copy.wait_recv()
    total = s4[section].astype(F32)
    for k in range(15):
        total = total + r4[k].astype(F32)
    grad_ref[0, :, wide:] = total.astype(BF16)

    for copy in started:
        copy.wait_send()


def hand_over(grad_ref, div_ref, grad_out, div_out):
    grad_out[...] = grad_ref[...]
    div_out[...] = div_ref[...]


N_SEM = 160


def body(hidden, head_weight, teacher_logprobs, lengths):
    width, vocab = head_weight.shape
    wide = 2 * NA
    V = pltpu.VMEM
    scratch = [
        V((width, vocab), BF16),
        V((8, 8, 8, vocab), F32),
        V((8, 8, 8, vocab), F32),
        pltpu.SMEM((4, 8), jnp.int32),
        V((NZ, 8, wide), BF16),
        V((16, 8, NB), BF16),
        V((NX, NY, 64, wide), BF16),
        V((NZ, LIVE, NB), BF16),
        V((NX, NY, 8, 8, vocab), F32),
        V((8, 8, 8, vocab), F32),
        V((3, 16, 128), F32),
        V((NZ - 1, 16, 128), F32),
        V((15, 16, 128), F32),
        V((NX, NY, 8, 8, vocab), BF16),
        V((2, 4, 4, 64, NA), BF16),
        V((2, 2, 2, 64, NA), F32),
        V((2, 4, 64, NA), F32),
        V((2, 2, 2, 64, NA), BF16),
        V((2, 2, 4, 64, NA), BF16),
        V((2, 3, 64, NA), BF16),
        V((2, 3, 64, NA), BF16),
        V((NZ, 8, wide), F32),
        V((NZ, 8, wide), BF16),
        V((NZ - 1, 8, wide), BF16),
        V((NZ, LIVE, NB), F32),
        V((2, 7, LIVE, HB), BF16),
        V((2, 7, LIVE, HB), BF16),
        V((16, 8, NB), BF16),
        V((15, 8, NB), BF16),
        pltpu.SemaphoreType.DMA((12,)),
        pltpu.SemaphoreType.DMA((N_SEM,)),
        pltpu.SemaphoreType.DMA((N_SEM,)),
    ]
    grad, divergence = pl.pallas_call(
        kernel,
        out_shape=(
            jax.ShapeDtypeStruct((1, 8, width), BF16),
            jax.ShapeDtypeStruct((1, 64), F32),
        ),
        in_specs=[
            pl.BlockSpec(memory_space=pl.ANY),
            pl.BlockSpec(memory_space=pl.ANY),
            pl.BlockSpec(memory_space=pl.ANY),
            pl.BlockSpec(memory_space=pl.ANY),
        ],
        out_specs=(pl.BlockSpec(memory_space=V), pl.BlockSpec(memory_space=V)),
        scratch_shapes=scratch,
        compiler_params=pltpu.CompilerParams(
            collective_id=0, has_side_effects=True, vmem_limit_bytes=56 * 1024 * 1024
        ),
        name="distill",
    )(hidden, head_weight, teacher_logprobs, lengths.T)
    return pl.pallas_call(
        hand_over,
        out_shape=(
            jax.ShapeDtypeStruct(grad.shape, grad.dtype),
            jax.ShapeDtypeStruct(divergence.shape, divergence.dtype),
        ),
        in_specs=[pl.BlockSpec(memory_space=V)] * 2,
        out_specs=(pl.BlockSpec(memory_space=V), pl.BlockSpec(memory_space=V)),
        name="hand_over",
    )(grad, divergence)


def solution(mesh):
    placed = (
        P("dp", "section", "tensor"),
        P("tensor", ("section", "dp")),
        P(None, "tensor", ("section", "dp")),
        P(),
    )
    return jax.shard_map(
        body,
        mesh=mesh,
        in_specs=placed,
        out_specs=(P("dp", "section", "tensor"), P("dp", "tensor")),
        check_vma=False,
    )
```

```python
import jax
import jax.numpy as jnp
from jax import lax
from jax.experimental import pallas as pl
from jax.experimental.pallas import tpu as pltpu
from jax.sharding import PartitionSpec as P

SEQ_MB, LIVE = 32, 80
NX, NY, NZ = 4, 4, 8
NA, NB = 512, 768
HB = NB // 2
F32, BF16 = jnp.float32, jnp.bfloat16


def kernel(
    hid_hbm, w_hbm, tl_hbm, len_hbm, grad_ref, div_ref,
    w, tl, tp, lengths, zb, pb, hb, hz, acc, lrecv, stats, rz, rp, g,
    s1, own1, r1f, s2, r2, u, s3, r3, prod, sb, rb, s4, r4,
    lsem, ssem, rsem,
):
    wide = NA + NA
    vocab = w.shape[1]
    section, z, t = lax.axis_index("section"), lax.axis_index("dp"), lax.axis_index("tensor")
    x, y = section // NY, section % NY
    other = 1 - t

    def at_x(k):
        return (((x + k) % NX) * NY + y, z, t)

    def at_y(k):
        return (x * NY + (y + k) % NY, z, t)

    def at_z(k):
        return (section, (z + k) % NZ, t)

    def plane(k):
        return ((x + k // NY) % NX) * NY + (y + k % NY) % NY

    def at_p(k):
        return (plane(k), z, t)

    far_z = (4, 3, 5, 2, 6, 1, 7)
    far_p = (10, 6, 14, 9, 11, 2, 8, 5, 7, 13, 15, 1, 3, 4, 12)
    partner = (section, z, other)
    started = []

    def send(src, dst, device):
        i = len(started)
        copy = pltpu.make_async_remote_copy(
            src_ref=src, dst_ref=dst, send_sem=ssem.at[i], recv_sem=rsem.at[i],
            device_id=device, device_id_type=pl.DeviceIdType.MESH,
        )
        copy.start()
        started.append(copy)
        return copy

    barrier = pltpu.get_barrier_semaphore()
    peers = [at_z(k) for k in far_z] + [at_p(k) for k in far_p] + [partner]
    for peer in peers:
        pl.semaphore_signal(barrier, inc=1, device_id=peer, device_id_type=pl.DeviceIdType.MESH)

    ca, cc, cac, cb = pl.ds(0, NA), pl.ds(NA, NA), pl.ds(0, wide), pl.ds(wide, NB)
    own_rows = (
        pltpu.make_async_copy(hid_hbm.at[0, :, cac], zb.at[z], lsem.at[10]),
        pltpu.make_async_copy(hid_hbm.at[0, :, cb], pb.at[section], lsem.at[11]),
    )
    for load in own_rows:
        load.start()

    loads = [pltpu.make_async_copy(w_hbm, w, lsem.at[0]), pltpu.make_async_copy(len_hbm, lengths, lsem.at[9])]
    for k in range(8):
        loads.append(pltpu.make_async_copy(tl_hbm.at[:, pl.ds(8 * k, 8), :], tl.at[k], lsem.at[k + 1]))
    for load in loads:
        load.start()
    for load in own_rows:
        load.wait()
    pl.semaphore_wait(barrier, len(peers))

    zs = [send(zb.at[z], zb.at[z], at_z(k)) for k in far_z]
    ps = [send(pb.at[section], pb.at[section], at_p(k)) for k in far_p]
    acc[...] = jnp.zeros_like(acc)
    loads[1].wait()

    def position(r, j):
        e1 = lengths[0, r]
        e2 = e1 + lengths[1, r]
        e3 = e2 + lengths[2, r]
        late = jnp.where(j >= e3, 3 * SEQ_MB - e3, 2 * SEQ_MB - e2)
        early = jnp.where(j >= e1, SEQ_MB - e1, 0)
        return j + jnp.where(j >= e2, late, early)

    def picked(r, rows):
        j = lax.broadcasted_iota(jnp.int32, (LIVE, 128), 0)
        p = lax.broadcasted_iota(jnp.int32, (LIVE, 128), 1)
        pick = (p == position(r, j)).astype(F32).astype(BF16)
        return jnp.dot(pick, rows, preferred_element_type=F32).astype(BF16)

    def put_back(r, rows):
        p = lax.broadcasted_iota(jnp.int32, (128, LIVE), 0)
        j = lax.broadcasted_iota(jnp.int32, (128, LIVE), 1)
        place = (p == position(r, j)).astype(F32).astype(BF16)
        return jnp.dot(place, rows, preferred_element_type=F32)

    for copy in zs:
        copy.wait_recv()
    hb[x, y] = zb[...].astype(F32).reshape(NZ * 8, wide).astype(BF16)
    ph2 = []
    for k in (2, 1, 3):
        ph2.append(send(hb.at[x, y, :, ca], hb.at[x, y, :, ca], at_y(k)))
        ph2.append(send(hb.at[x, y, :, cc], hb.at[x, y, :, cc], at_x(k)))
    for copy in ps:
        copy.wait_recv()
    hz[z] = picked(z, pb[...].astype(F32).reshape(128, NB).astype(BF16))

    def b_pass(step, right):
        i = (z - step) % NZ if right else (z + step) % NZ
        part = hz.at[i] if step < 3 else hz.at[i, :, pl.ds(0 if right else HB, HB)]
        return send(part, part, at_z(1 if right else NZ - 1))

    ring = [(b_pass(0, True), b_pass(0, False))]

    def b_forward(step):
        ring[step - 1][0].wait_recv()
        right = b_pass(step, True)
        ring[step - 1][1].wait_recv()
        ring.append((right, b_pass(step, False)))

    b_forward(1)

    for copy in ph2:
        copy.wait_recv()
    y1, y3, x1, x3 = (y + 1) % NY, (y + 3) % NY, (x + 1) % NX, (x + 3) % NX
    lo2, hi2 = pl.ds(0, 2), pl.ds(2, 2)

    def a_block(i, part):
        return hb.at[i, part, :, ca]

    def c_block(i, part):
        return hb.at[part, i, :, cc]

    ar0 = send(a_block(x, lo2), a_block(x, lo2), at_x(1))
    br0 = send(c_block(y, lo2), c_block(y, lo2), at_y(1))
    al0 = send(a_block(x, hi2), a_block(x, hi2), at_x(3))
    bl0 = send(c_block(y, hi2), c_block(y, hi2), at_y(3))
    ar1 = send(a_block(x, hi2), a_block(x, hi2), at_x(1))
    br1 = send(c_block(y, hi2), c_block(y, hi2), at_y(1))
    al1 = send(a_block(x, lo2), a_block(x, lo2), at_x(3))
    bl1 = send(c_block(y, lo2), c_block(y, lo2), at_y(3))

    def a_logits(i):
        rows = hb[i, :, :, 0:NA].reshape(256, NA)
        block = jnp.dot(rows, w[0:NA], preferred_element_type=F32)
        acc[i] = acc[i] + block.reshape(4, 8, 8, vocab)

    def c_logits(i):
        rows = hb[:, i, :, NA:wide].reshape(256, NA)
        block = jnp.dot(rows, w[NA:wide], preferred_element_type=F32)
        acc[:, i] = acc[:, i] + block.reshape(4, 8, 8, vocab)

    def b_logits(i):
        rows = put_back(i, hz[i]).astype(BF16)
        block = jnp.dot(rows, w[wide:], preferred_element_type=F32)
        acc[:, :, i] = acc[:, :, i] + block.reshape(4, 4, 8, vocab)

    def c_far(owner):
        rows = hb[pl.ds(2 * owner, 2), (y + 2) % NY, :, NA:wide].reshape(128, NA)
        block = jnp.dot(rows, w[NA:wide], preferred_element_type=F32)
        into = acc.at[pl.ds(2 * owner, 2), (y + 2) % NY]
        into[...] = into[...] + block.reshape(2, 8, 8, vocab)

    for load in [loads[0]] + loads[2:]:
        load.wait()

    def teacher_block(k, carry):
        tp[k] = jnp.exp(tl[k])
        return carry

    lax.fori_loop(0, 8, teacher_block, 0)
    b_logits(z)
    a_logits(x)
    c_logits(y)

    b_forward(2)
    b_logits((z + 1) % NZ)
    b_logits((z + 7) % NZ)
    ar0.wait_recv()
    ar2 = send(a_block(x3, lo2), a_block(x3, lo2), at_x(1))
    br0.wait_recv()
    br2 = send(c_block(y3, lo2), c_block(y3, lo2), at_y(1))
    al0.wait_recv()
    al2 = send(a_block(x1, hi2), a_block(x1, hi2), at_x(3))
    bl0.wait_recv()
    bl2 = send(c_block(y1, hi2), c_block(y1, hi2), at_y(3))
    b_forward(3)
    b_logits((z + 2) % NZ)
    b_logits((z + 6) % NZ)
    for copy in [ar1, br1, al1, bl1]:
        copy.wait_recv()
    for k in (1, 3):
        a_logits((x + k) % NX)
        c_logits((y + k) % NY)
    b_logits((z + 3) % NZ)
    b_logits((z + 5) % NZ)
    for copy in ring[3]:
        copy.wait_recv()
    b_logits((z + 4) % NZ)
    for copy in (ar2, al2):
        copy.wait_recv()
    a_logits((x + 2) % NX)
    for copy in (br2, bl2):
        copy.wait_recv()
    c_far(other)
    exchanges = []
    for k in range(4):
        block = acc.at[2 * other + k // 2, pl.ds(2 * (k % 2), 2)]
        exchanges.append(send(block, lrecv.at[pl.ds(2 * k, 2)], partner))
    c_far(t)

    row_i = lax.broadcasted_iota(jnp.int32, (128, 128), 0)
    lane_i = lax.broadcasted_iota(jnp.int32, (128, 128), 1)
    eye = row_i == lane_i

    def to_lanes(col):
        return jnp.sum(jnp.where(eye, col, 0.0), axis=0, keepdims=True)

    def to_rows(lane):
        return jnp.sum(jnp.where(eye, lane, 0.0), axis=1, keepdims=True)

    for k in range(4):
        exchanges[k].wait_recv()
        pair = slice(2 * k, 2 * k + 2)
        both = acc[2 * t + k // 2, 2 * (k % 2):2 * (k % 2) + 2] + lrecv[pair]
        lrecv[pair] = both
        logits = both.reshape(128, vocab)
        teacher = tl[pair].reshape(128, vocab)
        prob = tp[pair].reshape(128, vocab)
        top = jnp.max(logits, axis=1, keepdims=True)
        total = jnp.sum(jnp.exp(logits - top), axis=1, keepdims=True)
        cross = jnp.sum(prob * (teacher - logits), axis=1, keepdims=True)
        mass = jnp.sum(prob, axis=1, keepdims=True)
        stats[0, k:k + 1, :] = to_lanes(top)
        stats[0, 4 + k:5 + k, :] = to_lanes(total)
        stats[0, 8 + k:9 + k, :] = to_lanes(cross)
        stats[0, 12 + k:13 + k, :] = to_lanes(mass)

    for level, (slots, at, order) in enumerate(((rz, at_z, far_z), (rp, at_p, far_p))):
        copies = [send(stats.at[level], slots.at[k - 1], at(k)) for k in order]
        for copy in copies:
            copy.wait_recv()
        parts = [stats[level]] + [slots[k] for k in range(len(order))]
        top = parts[0][0:4]
        for part in parts[1:]:
            top = jnp.maximum(top, part[0:4])
        total = sum(part[4:8] * jnp.exp(part[0:4] - top) for part in parts)
        sums = sum(part[8:16] for part in parts)
        stats[level + 1, 0:4, :] = top
        stats[level + 1, 4:8, :] = total
        stats[level + 1, 8:16, :] = sums

    log_norm = stats[2, 0:4, :] + jnp.log(stats[2, 4:8, :])
    cross, mass = stats[2, 8:12, :], stats[2, 12:16, :]
    row_id = lax.broadcasted_iota(jnp.int32, (4, 128), 0) * 128 + lax.broadcasted_iota(jnp.int32, (4, 128), 1)
    local_section, replica, inner = row_id // 64, (row_id // 8) % 8, row_id % 8
    within = (local_section % 4) * 8 + inner
    micro = local_section // 4
    chosen = jnp.ones((4, 128), jnp.int32)
    for r in range(NZ):
        for m in range(2):
            length = jnp.where(t == 0, lengths[m, r], lengths[m + 2, r])
            chosen = jnp.where((replica == r) & (micro == m), length, chosen)
    live = (within < chosen).astype(F32)
    weight = live * (SEQ_MB / chosen.astype(F32))
    divergence = live * (cross + log_norm * mass)
    scale = weight * mass

    div_total = jnp.zeros((1, 128), F32)
    swaps = []
    for k in range(4):
        norm_rows = to_rows(log_norm[k:k + 1])
        scale_rows = to_rows(scale[k:k + 1])
        weight_rows = to_rows(weight[k:k + 1])
        pair = slice(2 * k, 2 * k + 2)
        logits = lrecv[pair].reshape(128, vocab)
        prob = tp[pair].reshape(128, vocab)
        grad = jnp.exp(logits - norm_rows) * scale_rows - weight_rows * prob
        g[2 * t + k // 2, 2 * (k % 2):2 * (k % 2) + 2] = grad.reshape(2, 8, 8, vocab).astype(BF16)
        mine = g.at[2 * t + k // 2, pl.ds(2 * (k % 2), 2)]
        swaps.append(send(mine, mine, partner))
    for k in range(4):
        div_rows = to_rows(divergence[k:k + 1])
        place = (2 * k + row_i // 64) * 8 + row_i % 8
        pick = (lane_i == place) & ((row_i // 8) % 8 == z)
        div_total = div_total + jnp.sum(jnp.where(pick, div_rows, 0.0), axis=0, keepdims=True)
    div_ref[...] = div_total[:, 0:64]
    for copy in swaps:
        copy.wait_recv()

    def times_w(rows, start, size):
        return lax.dot_general(
            rows, w[start:start + size, :], (((1,), (1,)), ((), ())), preferred_element_type=F32
        )

    def product(part, o):
        rows = g[(x + o) % NX] if part == 0 else g[:, (y + o) % NY]
        rows = rows.astype(F32).reshape(256, vocab).astype(BF16)
        return times_w(rows, part * NA, NA).reshape(4, 64, NA)

    def b_product(o):
        i = (z + o) % NZ
        rows = g[:, :, i].astype(F32).reshape(128, vocab).astype(BF16)
        prod[i] = times_w(picked(i, rows), wide, NB)

    first = (at_x, at_y)
    second = (at_y, at_x)
    halves = (slice(0, HB), slice(HB, NB))

    def b_item(side, item, extra=None):
        step = 0 if item == 0 else (item + 1) // 2
        upper = (item % 2 == 0) if side == 0 else (item % 2 == 1)
        owner = (z + 4 - step) % NZ if side == 0 else (z + 4 + step) % NZ
        value = prod[owner, :, halves[0 if upper else 1]]
        if extra is not None:
            value = value + extra
        sb[side, item] = value.astype(BF16)
        return send(sb.at[side, item], rb.at[side, item], at_z(1 if side == 0 else NZ - 1))

    direct = []

    def direct_sum(o):
        for part in range(2):
            s1[part, o - 1] = product(part, o).astype(BF16)
            direct.append(send(s1.at[part, o - 1], r1f.at[part, o - 1], first[part](o)))

    direct_sum(2)
    b_product(4)
    sides = [[b_item(side, 0)] for side in range(2)]
    def b_next(item):
        source = 0 if item == 2 else item - 2
        for side in range(2):
            sides[side][source].wait_recv()
            sides[side].append(b_item(side, item, rb[side, source].astype(F32)))

    direct_sum(1)
    direct_sum(3)
    for side in range(2):
        b_product((3, 5)[side])
        sides[side].append(b_item(side, 1))
    b_next(2)
    b_product(2)
    b_product(6)
    b_next(3)
    b_product(1)
    b_product(7)
    b_product(0)
    for part in range(2):
        own1[part] = product(part, 0)
    b_next(4)
    b_next(5)
    for copy in direct:
        copy.wait_recv()
    place2 = (y, x)
    ph2 = []
    for k in (2, 1, 3):
        for part in range(2):
            i = (place2[part] + k) % 4
            value = own1[part, i] + sum(r1f[part, j, i].astype(F32) for j in range(3))
            s2[part, k - 1] = value.astype(BF16)
            ph2.append(send(s2.at[part, k - 1], r2.at[part, k - 1], second[part](k)))
    b_next(6)
    for copy in ph2:
        copy.wait_recv()
    for part in range(2):
        i = place2[part]
        value = own1[part, i] + sum(r1f[part, j, i].astype(F32) for j in range(3))
        for k in range(3):
            value = value + r2[part, k].astype(F32)
        u[:, :, part * NA:(part + 1) * NA] = value.reshape(NZ, 8, NA)
    s3[...] = u[...].astype(BF16)
    zs = [send(s3.at[(z + k) % NZ], r3.at[k - 1], at_z(k)) for k in far_z]
    for side in range(2):
        for item in (5, 6):
            sides[side][item].wait_recv()
    b_first = prod[z, :, halves[0]] + rb[0, 6].astype(F32) + rb[1, 5].astype(F32)
    b_second = prod[z, :, halves[1]] + rb[0, 5].astype(F32) + rb[1, 6].astype(F32)
    live_rows = jnp.concatenate([b_first.astype(BF16), b_second.astype(BF16)], axis=1)
    s4[...] = put_back(z, live_rows).reshape(16, 8, NB).astype(BF16)
    ps = [send(s4.at[plane(k)], r4.at[k - 1], at_p(k)) for k in far_p]
    for copy in zs:
        copy.wait_recv()
    total = u[z]
    for k in range(NZ - 1):
        total = total + r3[k].astype(F32)
    grad_ref[0, :, 0:wide] = total.astype(BF16)
    for copy in ps:
        copy.wait_recv()
    total = s4[section].astype(F32)
    for k in range(15):
        total = total + r4[k].astype(F32)
    grad_ref[0, :, wide:] = total.astype(BF16)

    for copy in started:
        copy.wait_send()


def hand_over(grad_ref, div_ref, grad_out, div_out):
    grad_out[...] = grad_ref[...]
    div_out[...] = div_ref[...]


N_SEM = 160


def body(hidden, head_weight, teacher_logprobs, lengths):
    width, vocab = head_weight.shape
    wide = 2 * NA
    V = pltpu.VMEM
    scratch = [
        V((width, vocab), BF16),
        V((8, 8, 8, vocab), F32),
        V((8, 8, 8, vocab), F32),
        pltpu.SMEM((4, 8), jnp.int32),
        V((NZ, 8, wide), BF16),
        V((16, 8, NB), BF16),
        V((NX, NY, 64, wide), BF16),
        V((NZ, LIVE, NB), BF16),
        V((NX, NY, 8, 8, vocab), F32),
        V((8, 8, 8, vocab), F32),
        V((3, 16, 128), F32),
        V((NZ - 1, 16, 128), F32),
        V((15, 16, 128), F32),
        V((NX, NY, 8, 8, vocab), BF16),
        V((2, 3, 4, 64, NA), BF16),
        V((2, 4, 64, NA), F32),
        V((2, 3, 4, 64, NA), BF16),
        V((2, 3, 64, NA), BF16),
        V((2, 3, 64, NA), BF16),
        V((NZ, 8, wide), F32),
        V((NZ, 8, wide), BF16),
        V((NZ - 1, 8, wide), BF16),
        V((NZ, LIVE, NB), F32),
        V((2, 7, LIVE, HB), BF16),
        V((2, 7, LIVE, HB), BF16),
        V((16, 8, NB), BF16),
        V((15, 8, NB), BF16),
        pltpu.SemaphoreType.DMA((12,)),
        pltpu.SemaphoreType.DMA((N_SEM,)),
        pltpu.SemaphoreType.DMA((N_SEM,)),
    ]
    grad, divergence = pl.pallas_call(
        kernel,
        out_shape=(
            jax.ShapeDtypeStruct((1, 8, width), BF16),
            jax.ShapeDtypeStruct((1, 64), F32),
        ),
        in_specs=[
            pl.BlockSpec(memory_space=pl.ANY),
            pl.BlockSpec(memory_space=pl.ANY),
            pl.BlockSpec(memory_space=pl.ANY),
            pl.BlockSpec(memory_space=pl.ANY),
        ],
        out_specs=(pl.BlockSpec(memory_space=V), pl.BlockSpec(memory_space=V)),
        scratch_shapes=scratch,
        compiler_params=pltpu.CompilerParams(
            collective_id=0, has_side_effects=True, vmem_limit_bytes=56 * 1024 * 1024
        ),
        name="distill",
    )(hidden, head_weight, teacher_logprobs, lengths.T)
    return pl.pallas_call(
        hand_over,
        out_shape=(
            jax.ShapeDtypeStruct(grad.shape, grad.dtype),
            jax.ShapeDtypeStruct(divergence.shape, divergence.dtype),
        ),
        in_specs=[pl.BlockSpec(memory_space=V)] * 2,
        out_specs=(pl.BlockSpec(memory_space=V), pl.BlockSpec(memory_space=V)),
        name="hand_over",
    )(grad, divergence)


def solution(mesh):
    placed = (
        P("dp", "section", "tensor"),
        P("tensor", ("section", "dp")),
        P(None, "tensor", ("section", "dp")),
        P(),
    )
    return jax.shard_map(
        body,
        mesh=mesh,
        in_specs=placed,
        out_specs=(P("dp", "section", "tensor"), P("dp", "tensor")),
        check_vma=False,
    )
```
